32 devices in a mesh: fsdp: 32 (over z, y, x, core).
Axes of the slice: x: 2, y: 2, z: 4, core: 2. Of those that a mesh axis runs over, the one named last changes fastest.
Arguments:
- tokens: bfloat16 [12608, 768], P('fsdp'), may hold values from -6 to 6
- cotangent: bfloat16 [12608, 768], P('fsdp'), may hold values from -6 to 6
- expert_ids: int32 [12608, 2], P('fsdp'), may hold values from 0 to 3, as said below
- slots: int32 [12608, 2], P('fsdp'), may hold values from 0 to 245, as said below
- norm1_gain: bfloat16 [768], P('fsdp'), may hold values from 0.5 to 1.5
- norm1_shift: bfloat16 [768], P('fsdp'), may hold values from -1.75 to 1.75
- query_weight: bfloat16 [768, 768], P('fsdp'), may hold values from -0.21875 to 0.21875
- query_bias: bfloat16 [768], P('fsdp'), may hold values from -1.75 to 1.75
- key_weight: bfloat16 [768, 768], P('fsdp'), may hold values from -0.21875 to 0.21875
- value_weight: bfloat16 [768, 768], P('fsdp'), may hold values from -0.21875 to 0.21875
- value_bias: bfloat16 [768], P('fsdp'), may hold values from -1.75 to 1.75
- out_weight: bfloat16 [768, 768], P('fsdp'), may hold values from -0.875 to 0.875
- out_bias: bfloat16 [768], P('fsdp'), may hold values from -1.75 to 1.75
- norm2_gain: bfloat16 [768], P('fsdp'), may hold values from 0.5 to 1.5
- norm2_shift: bfloat16 [768], P('fsdp'), may hold values from -1.75 to 1.75
- router_weight: bfloat16 [768, 4], P('fsdp'), may hold values from -0.15625 to 0.15625
- expert_in: bfloat16 [4, 768, 3072], P(None, 'fsdp'), may hold values from -0.21875 to 0.21875
- expert_in_bias: bfloat16 [4, 3072], P(None, 'fsdp'), may hold values from -1.75 to 1.75
- expert_out: bfloat16 [4, 3072, 768], P(None, 'fsdp'), may hold values from -0.109375 to 0.109375
- expert_out_bias: bfloat16 [4, 768], P(None, 'fsdp'), may hold values from -1.75 to 1.75
Outputs:
- mixed_out: bfloat16 [12608, 768], P('fsdp')
- tokens_grad: float32 [12608, 768], P('fsdp')
- norm1_gain_grad: float32 [768], P('fsdp')
- norm1_shift_grad: float32 [768], P('fsdp')
- query_weight_grad: float32 [768, 768], P('fsdp')
- query_bias_grad: float32 [768], P('fsdp')
- key_weight_grad: float32 [768, 768], P('fsdp')
- value_weight_grad: float32 [768, 768], P('fsdp')
- value_bias_grad: float32 [768], P('fsdp')
- out_weight_grad: float32 [768, 768], P('fsdp')
- out_bias_grad: float32 [768], P('fsdp')
- norm2_gain_grad: float32 [768], P('fsdp')
- norm2_shift_grad: float32 [768], P('fsdp')
- router_weight_grad: float32 [768, 4], P('fsdp')
- expert_in_grad: float32 [4, 768, 3072], P(None, 'fsdp')
- expert_in_bias_grad: float32 [4, 3072], P(None, 'fsdp')
- expert_out_grad: float32 [4, 3072, 768], P(None, 'fsdp')
- expert_out_bias_grad: float32 [4, 768], P(None, 'fsdp')
The draws below stay inside these ranges and needn't reach their ends.
Inputs may be any that keep to these rules, and one draw needn't show every extreme that they name: `expert_ids`: each token's two experts differ. `slots`: among one device's tokens no two choices share both expert and slot, so an expert takes at most 246 of one device's choices; on every device some expert takes exactly 246.
All inputs are finite; a program needn't handle non-finite values.
Results may differ from the reference program's by a relative error of at most 0.029.
Values may be sent and summed in bfloat16 or wider, within the bound.
No kernel may reach another device: no remote copies, remote signals or barrier semaphores. Data moves between devices by JAX's collectives and lax.ppermute only.
A program may use at most 320 MiB of HBM per device.

```python
import jax
import jax.numpy as jnp
from jax import lax

D = 768
HEADS = 12
HEAD_DIM = 64
FF = 3072
EXP = 4
SEQ = 197
TOK_DEV = 394
CAP = 246
TOKENS = 12608
N_FSDP = 32


def route_device(key):
    key_list = jax.random.split(key, 5)
    busy_expert = jax.random.randint(key_list[0], (), 0, EXP)
    token_order = jax.random.permutation(key_list[1], TOK_DEV)
    position = jnp.argsort(token_order).astype(jnp.int32)
    full_cols = TOK_DEV - CAP
    in_full = position < 2 * full_cols
    column = jnp.where(in_full, position // 2, position - full_cols)
    second_role = jnp.logical_and(in_full, position % 2 == 1)
    column_picks = jax.random.randint(key_list[2], (CAP,), 0, EXP - 1)
    col_pick = column_picks[column]
    first_pick = jnp.where(second_role, (busy_expert + 1 + (col_pick + 1) % (EXP - 1)) % EXP, busy_expert)
    second = jnp.where(second_role, (busy_expert + 1 + (col_pick + 2) % (EXP - 1)) % EXP, (busy_expert + 1 + col_pick) % EXP)
    slot_orders = jax.vmap(lambda sub_key: jax.random.permutation(sub_key, CAP))(jax.random.split(key_list[3], EXP))
    slot_first = slot_orders[first_pick, column]
    slot_second = slot_orders[second, column]
    swapped = jax.random.randint(key_list[4], (TOK_DEV,), 0, 2) == 1
    chosen_ids = jnp.stack([jnp.where(swapped, second, first_pick), jnp.where(swapped, first_pick, second)], -1)
    slot_pos = jnp.stack([jnp.where(swapped, slot_second, slot_first), jnp.where(swapped, slot_first, slot_second)], -1)
    return (chosen_ids.astype(jnp.int32), slot_pos.astype(jnp.int32))


def routing(key):
    devices = TOKENS // TOK_DEV
    dev_keys = jax.vmap(lambda device_index: jax.random.fold_in(key, device_index))(jnp.arange(devices))
    chosen_ids, slot_pos = jax.vmap(route_device)(dev_keys)
    return (chosen_ids.reshape(TOKENS, 2), slot_pos.reshape(TOKENS, 2))


def draw_expert_ids(key, part):
    return routing(key)[0]


def draw_slots(key, part):
    return routing(key)[1]


def steps_of(own_key, shape, cuts, smallest, largest):
    def one(axis_at, blocks):
        steps = jax.random.uniform(jax.random.fold_in(jax.random.fold_in(own_key, 6), axis_at), (blocks,), jnp.float32, smallest / len(cuts), largest / len(cuts))
        return jnp.repeat(jnp.exp(steps), shape[axis_at] // blocks).reshape((-1,) + (1,) * (len(shape) - axis_at - 1))

    loudness = one(*cuts[0])
    for cut in cuts[1:]:
        loudness = loudness * one(*cut)
    return loudness


def noise(own_key, dims, width, most, cuts=(), held_as=jnp.bfloat16):
    values = width * jax.random.normal(own_key, dims, jnp.float32)
    if cuts:
        values = values * steps_of(own_key, dims, cuts, -0.22, 0.18)
    return jnp.clip(values, -most, most).astype(held_as)


def setup_inputs(seed: int = 0) -> dict:
    keys = jax.random.split(jax.random.key(seed), 21)
    return {
        "tokens": noise(keys[0], (TOKENS, D), 1.0, 6.0, ((0, 32),)),
        "cotangent": noise(keys[1], (TOKENS, D), 1.0, 6.0, ((0, 32),)),
        "expert_ids": draw_expert_ids(jax.random.fold_in(keys[20], 71), 0),
        "slots": draw_slots(jax.random.fold_in(keys[20], 71), 0),
        "norm1_gain": jnp.clip(1.0 + 0.1 * jax.random.normal(keys[4], (D,), jnp.float32), 0.5, 1.5).astype(jnp.bfloat16),
        "norm1_shift": noise(keys[5], (D,), 0.3, 1.75, ((0, 32),)),
        "query_weight": noise(keys[6], (D, D), D ** -0.5, 0.21875, ((0, 32),)),
        "query_bias": noise(keys[7], (D,), 0.3, 1.75, ((0, 32),)),
        "key_weight": noise(keys[8], (D, D), D ** -0.5, 0.21875, ((0, 32),)),
        "value_weight": noise(keys[9], (D, D), D ** -0.5, 0.21875, ((0, 32),)),
        "value_bias": noise(keys[10], (D,), 0.3, 1.75, ((0, 32),)),
        "out_weight": noise(keys[11], (D, D), (D // 16) ** -0.5, 0.875, ((0, 32),)),
        "out_bias": noise(keys[12], (D,), 0.3, 1.75, ((0, 32),)),
        "norm2_gain": jnp.clip(1.0 + 0.1 * jax.random.normal(keys[13], (D,), jnp.float32), 0.5, 1.5).astype(jnp.bfloat16),
        "norm2_shift": noise(keys[14], (D,), 0.3, 1.75, ((0, 32),)),
        "router_weight": noise(keys[15], (D, EXP), 0.025, 0.15625, ((0, 32),)),
        "expert_in": noise(keys[16], (EXP, D, FF), D ** -0.5, 0.21875, ((1, 32),)),
        "expert_in_bias": noise(keys[17], (EXP, FF), 0.3, 1.75, ((1, 32),)),
        "expert_out": noise(keys[18], (EXP, FF, D), FF ** -0.5, 0.109375, ((1, 32),)),
        "expert_out_bias": noise(keys[19], (EXP, D), 0.3, 1.75, ((1, 32),)),
    }


EPSILON = 1e-05
SCALE = 0.125

@jax.custom_vjp
def low(v):
    return lax.optimization_barrier(v.astype(jnp.bfloat16)).astype(jnp.float32)

@jax.custom_vjp
def low_back(v):
    return v

def low_keep(v):
    return (low(v), None)

def low_pass(kept, grad):
    return (grad,)

def back_keep(v):
    return (v, None)

def back_low(kept, grad):
    return (low(grad),)
low.defvjp(low_keep, low_pass)
low_back.defvjp(back_keep, back_low)

def norm_rows(values, gain, shift):
    mean_row = lax.optimization_barrier(jnp.mean(values, -1, keepdims=True))
    centred = values - mean_row
    variance = lax.optimization_barrier(jnp.mean(centred * centred, -1, keepdims=True))
    return centred * lax.rsqrt(variance + EPSILON) * gain + shift

def smooth_gelu(inner):
    return 0.5 * inner * (1.0 + jnp.tanh(0.7978845608 * (inner + 0.044715 * inner * inner * inner)))

def soft_max(values):
    row_max = lax.optimization_barrier(jnp.max(values, -1, keepdims=True))
    raised = jnp.exp(values - row_max)
    return raised / lax.optimization_barrier(jnp.sum(raised, -1, keepdims=True))

def device_layer(x_rows, id_rows, slot_rows, params):
    gain_one, shift_one, w_query, b_query, w_key, w_value, b_value, w_out, b_out, gain_two, shift_two, w_router, w_in, b_in, w_exit, b_exit = params
    highest = lax.Precision.HIGHEST
    tok_rows = x_rows.shape[0]
    images = tok_rows // SEQ
    normed_a = low(norm_rows(x_rows, gain_one, shift_one))
    query = low(low_back(jnp.dot(normed_a, w_query, precision=highest) + b_query))
    keys_all = low(low_back(jnp.dot(normed_a, w_key, precision=highest)))
    values_all = low(low_back(jnp.dot(normed_a, w_value, precision=highest) + b_value))
    heads_shape = (images, SEQ, HEADS, HEAD_DIM)
    scores = low_back(jnp.einsum('ishd,ithd->ihst', query.reshape(heads_shape), keys_all.reshape(heads_shape), precision=highest) * SCALE)
    probs = low(soft_max(scores))
    attended = jnp.einsum('ihst,ithd->ishd', probs, values_all.reshape(heads_shape), precision=highest)
    attended = low(low_back(attended.reshape(tok_rows, D)))
    branch_a = low_back(jnp.dot(attended, w_out, precision=highest) + b_out)
    resid = x_rows + branch_a
    normed_b = low(norm_rows(resid, gain_two, shift_two))
    logits = low_back(jnp.dot(normed_b, w_router, precision=highest))
    one_hot = (id_rows[:, :, None] == jnp.arange(EXP, dtype=jnp.int32)[None, None, :]).astype(jnp.float32)
    chosen = jnp.einsum('te,tke->tk', logits, one_hot, precision=highest)
    gates = soft_max(chosen)
    cell_index = (id_rows * CAP + slot_rows).astype(jnp.int32)
    blocks = jnp.zeros((EXP * CAP, D), jnp.float32).at[cell_index.reshape(-1)].set(jnp.repeat(normed_b, 2, axis=0))
    blocks = blocks.reshape(EXP, CAP, D)
    inner = low_back(jnp.einsum('ecd,edf->ecf', blocks, w_in, precision=highest) + b_in[:, None, :])
    activ = low(smooth_gelu(inner))
    expert_y = low_back(jnp.einsum('ecf,efd->ecd', activ, w_exit, precision=highest) + b_exit[:, None, :])
    picked = expert_y.reshape(EXP * CAP, D)[cell_index]
    return resid + jnp.einsum('tk,tkd->td', gates, picked, precision=highest)

def reference(tokens, cotangent, expert_ids, slots, norm1_gain, norm1_shift, query_weight, query_bias, key_weight, value_weight, value_bias, out_weight, out_bias, norm2_gain, norm2_shift, router_weight, expert_in, expert_in_bias, expert_out, expert_out_bias):
    params = tuple((item.astype(jnp.float32) for item in (norm1_gain, norm1_shift, query_weight, query_bias, key_weight, value_weight, value_bias, out_weight, out_bias, norm2_gain, norm2_shift, router_weight, expert_in, expert_in_bias, expert_out, expert_out_bias)))
    x_all = tokens.astype(jnp.float32)
    id_all = expert_ids.reshape(N_FSDP, TOK_DEV, 2)
    slot_all = slots.reshape(N_FSDP, TOK_DEV, 2)
    layer_ckpt = jax.checkpoint(device_layer)

    def whole(x_in, weights):

        def per_device(pieces):
            return layer_ckpt(pieces[0], pieces[1], pieces[2], weights)
        outputs = lax.map(per_device, (x_in.reshape(N_FSDP, TOK_DEV, D), id_all, slot_all))
        return outputs.reshape(TOKENS, D)
    result, backward = jax.vjp(whole, x_all, params)
    x_grad, grads = backward(cotangent.astype(jnp.float32))
    return (result.astype(jnp.bfloat16), x_grad, grads[0], grads[1], grads[2], grads[3], grads[4], grads[5], grads[6], grads[7], grads[8], grads[9], grads[10], grads[11], grads[12], grads[13], grads[14], grads[15])
```

```python
import functools

import jax
import jax.numpy as jnp
from jax import lax
from jax.experimental import pallas as pl
from jax.experimental.pallas import tpu as pltpu
from jax.sharding import PartitionSpec as P

D = 768
HEADS = 12
HEAD_DIM = 64
EXP = 4
SEQ = 197
CAP = 246
CELLS = 256


EPSILON = 1e-05
SCALE = 0.125
F32 = jnp.float32
BF16 = jnp.bfloat16
AXIS = "fsdp"

GROUP_BITS = (0, 3)


def group_mask(k):
    return (k & 1) << GROUP_BITS[0] | (k >> 1) << GROUP_BITS[1]


def norm_rows(values, gain, shift):
    mean_row = jnp.mean(values, -1, keepdims=True)
    centred = values - mean_row
    rstd_row = lax.rsqrt(jnp.mean(centred * centred, -1, keepdims=True) + EPSILON)
    unit_rows = centred * rstd_row
    return (unit_rows * gain + shift, unit_rows, rstd_row)


def norm_back(grad_in, unit_rows, rstd_row, gain):
    scaled = grad_in * gain
    input_grad = rstd_row * (
        scaled
        - jnp.mean(scaled, -1, keepdims=True)
        - unit_rows * jnp.mean(scaled * unit_rows, -1, keepdims=True)
    )
    return (input_grad, jnp.sum(grad_in * unit_rows, 0), jnp.sum(grad_in, 0))


def smooth_gelu(inner):
    return 0.5 * inner * (1.0 + jnp.tanh(0.7978845608 * (inner + 0.044715 * inner * inner * inner)))


def swap(x, n, mask):
    return lax.ppermute(x, AXIS, [(i, i ^ mask) for i in range(n)])


def bit_of(me, bit):
    return (me >> bit) & 1


def gather_all(x, n, me, order):
    width = n.bit_length() - 1
    x = x.reshape((1,) * width + x.shape)
    for bit in order:
        axis = width - 1 - bit
        other = swap(x, n, 1 << bit)
        high = bit_of(me, bit) == 1
        x = jnp.concatenate([jnp.where(high, other, x), jnp.where(high, x, other)], axis)
    return x.reshape((n,) + x.shape[width:])


def halve(x, n, me, bit, axis):
    mine = bit_of(me, bit)
    send = lax.dynamic_index_in_dim(x, 1 - mine, axis, keepdims=True)
    keep = lax.dynamic_index_in_dim(x, mine, axis, keepdims=True)
    other = swap(send, n, 1 << bit)
    return (keep.astype(F32) + other.astype(F32)).astype(BF16)


def scatter_sum(x, n, me, order):
    width = n.bit_length() - 1
    tail = x.shape[1:]
    x = x.reshape((2,) * width + tail)
    for bit in order:
        x = halve(x, n, me, bit, width - 1 - bit)
    return x.reshape(tail)


def place_kernel(masks, pair_rows, me_ref, *refs):
    pieces, out, sems = refs[: len(masks)], refs[len(masks)], refs[len(masks) + 1]
    copies = []
    for j, mask in enumerate(masks):
        for z in range(2):
            pair = (me_ref[0] ^ (mask | z << GROUP_BITS[1])) >> 1
            copies.append(
                pltpu.make_async_copy(
                    pieces[j].at[z],
                    out.at[pl.ds(pl.multiple_of(pair * pair_rows, pair_rows), pair_rows)],
                    sems.at[2 * j + z],
                )
            )
    for copy in copies:
        copy.start()
    for copy in copies:
        copy.wait()


def place(pieces, n, me):
    masks = sorted(pieces)
    _, pair_rows, columns = pieces[0].shape
    rows = pair_rows * (n // 2)
    if pair_rows % 16 == 0:
        return pl.pallas_call(
            functools.partial(place_kernel, masks, pair_rows),
            out_shape=jax.ShapeDtypeStruct((rows, columns), BF16),
            in_specs=[pl.BlockSpec(memory_space=pltpu.SMEM)]
            + [pl.BlockSpec(memory_space=pl.ANY)] * len(masks),
            out_specs=pl.BlockSpec(memory_space=pl.ANY),
            scratch_shapes=[pltpu.SemaphoreType.DMA((2 * len(masks),))],
        )(me.reshape(1).astype(jnp.int32), *[pieces[mask] for mask in masks])
    by_mask = [None] * (n // 2)
    for mask in masks:
        for z in range(2):
            by_mask[(mask | z << GROUP_BITS[1]) >> 1] = pieces[mask][z]
    order = jnp.arange(n // 2, dtype=jnp.int32) ^ (me >> 1)
    return jnp.take(jnp.stack(by_mask), order, axis=0).reshape(rows, columns)


def expert_gather(shard, n, me, expert, order):
    own = [
        lax.dynamic_index_in_dim(shard, expert ^ k, 0, keepdims=False) for k in range(EXP)
    ]
    got = [own[0]] + [swap(own[k], n, group_mask(k)) for k in range(1, EXP)]
    high = bit_of(me, GROUP_BITS[0]) == 1
    rows, columns = shard.shape[1:]
    block = jnp.stack(
        [
            jnp.stack([jnp.where(high, odd, even), jnp.where(high, even, odd)])
            for even, odd in ((got[0], got[1]), (got[2], got[3]))
        ]
    ).reshape(2, 2 * rows, columns)
    pieces = {0: block}
    for bit in order:
        for mask in list(pieces):
            pieces[mask | 1 << bit] = swap(pieces[mask], n, 1 << bit)
    return place(pieces, n, me)


def expert_scatter(grad, n, me, expert, order):
    width = n.bit_length() - 1
    rows, columns = grad.shape[0] // n, grad.shape[1]
    x = grad.reshape((2,) * width + (rows, columns))
    for bit in order:
        x = halve(x, n, me, bit, width - 1 - bit)
    x = x.reshape(2, 2, rows, columns)
    own_z, own_c = bit_of(me, GROUP_BITS[1]), bit_of(me, GROUP_BITS[0])
    got = []
    for k in range(EXP):
        part = lax.dynamic_slice(
            x, (own_z ^ (k >> 1), own_c ^ (k & 1), 0, 0), (1, 1, rows, columns)
        ).reshape(rows, columns)
        got.append(part if k == 0 else swap(part, n, group_mask(k)))
    places = jnp.arange(EXP, dtype=jnp.int32) ^ expert
    return jnp.stack(
        [
            lax.select_n(places[i], *got).astype(F32)
            for i in range(EXP)
        ]
    )


def per_device(
    n,
    tokens,
    cotangent,
    expert_ids,
    slots,
    norm1_gain,
    norm1_shift,
    query_weight,
    query_bias,
    key_weight,
    value_weight,
    value_bias,
    out_weight,
    out_bias,
    norm2_gain,
    norm2_shift,
    router_weight,
    expert_in,
    expert_in_bias,
    expert_out,
    expert_out_bias,
):
    me = lax.axis_index(AXIS)
    width = n.bit_length() - 1
    expert = bit_of(me, GROUP_BITS[0]) | bit_of(me, GROUP_BITS[1]) << 1
    far_bits = [b for b in range(width) if b not in GROUP_BITS and b > 2][::-1]
    x_first = far_bits + [1, 2]
    y_first = far_bits + [2, 1]
    rows = query_weight.shape[0]
    ff_rows = expert_out.shape[1]
    ff = ff_rows * n
    tok_rows = tokens.shape[0]
    images = tok_rows // SEQ
    heads_shape = (images, SEQ, HEADS, HEAD_DIM)

    vectors = jnp.stack(
        [norm1_gain, norm1_shift, query_bias, value_bias, out_bias, norm2_gain, norm2_shift]
    )
    small = jnp.concatenate(
        [vectors, router_weight.T, expert_out_bias], 0
    ).reshape(-1)
    small = jnp.concatenate([small, expert_in_bias.reshape(-1)])
    n_small = small.shape[0]
    small = jnp.pad(small, (0, D - n_small)).reshape(1, D)
    pack_a = jnp.concatenate([query_weight, key_weight], 0)
    pack_b = jnp.concatenate([value_weight, out_weight, small], 0)
    full_a = gather_all(pack_a, n, me, far_bits + [3, 1, 2, 0])
    full_b = gather_all(pack_b, n, me, far_bits + [3, 2, 1, 0])
    w_query = full_a[:, :rows].reshape(D, D)
    w_key = full_a[:, rows:].reshape(D, D)
    w_value = full_b[:, :rows].reshape(D, D)
    w_out = full_b[:, rows : 2 * rows].reshape(D, D)
    small_full = full_b[:, 2 * rows]
    vec = small_full[:, : 15 * rows].reshape(n, 15, rows).transpose(1, 0, 2).reshape(15, D)
    gain_one, shift_one, b_query, b_value, b_out, gain_two, shift_two = [
        vec[i].astype(F32) for i in range(7)
    ]
    w_router_t = vec[7:11]
    b_exit = lax.dynamic_index_in_dim(vec[11:15], expert, 0, keepdims=True).astype(F32)
    b_in_all = small_full[:, 15 * rows : n_small].reshape(n, EXP, ff_rows)
    b_in = lax.dynamic_index_in_dim(b_in_all, expert, 1, keepdims=False).reshape(1, ff).astype(F32)

    w_in = expert_gather(expert_in, n, me, expert, x_first)
    w_exit = expert_gather(expert_out, n, me, expert, y_first)

    cell_index = (expert_ids ^ expert) * CELLS + slots
    cell_ids = jnp.arange(EXP * CELLS, dtype=jnp.int32)
    hit_rows = [
        (cell_index[:, k][None, :] == cell_ids[:, None]) for k in range(2)
    ]
    spread = (hit_rows[0] | hit_rows[1]).astype(BF16)
    cot_cells = jnp.dot(spread, cotangent, preferred_element_type=F32).astype(BF16)

    def to_experts(cells):
        parts = cells.reshape((EXP, CELLS) + cells.shape[1:])
        return jnp.concatenate(
            [parts[0]] + [swap(parts[k], n, group_mask(k)) for k in range(1, EXP)], 0
        )

    cot_blocks = to_experts(cot_cells)

    inputs = tokens.astype(F32)
    normed_a, unit_a, rstd_a = norm_rows(inputs, gain_one, shift_one)
    hidden_a = normed_a.astype(BF16)
    query = (jnp.dot(hidden_a, w_query, preferred_element_type=F32) + b_query).astype(BF16)
    keys_all = jnp.dot(hidden_a, w_key, preferred_element_type=F32).astype(BF16)
    values_all = (jnp.dot(hidden_a, w_value, preferred_element_type=F32) + b_value).astype(BF16)
    query_h = query.reshape(heads_shape)
    key_h = keys_all.reshape(heads_shape)
    value_h = values_all.reshape(heads_shape)
    scores = jnp.einsum("ishd,ithd->ihst", query_h, key_h, preferred_element_type=F32) * SCALE
    row_max = jnp.max(scores, -1, keepdims=True)
    raised = jnp.exp(scores - row_max)
    row_total = jnp.sum(raised, -1, keepdims=True)
    probs = raised / row_total
    log_total = row_max + jnp.log(row_total)
    mixed_h = jnp.einsum("ihst,ithd->ishd", probs.astype(BF16), value_h, preferred_element_type=F32)
    attended = mixed_h.astype(BF16).reshape(tok_rows, D)
    branch_a = jnp.dot(attended, w_out, preferred_element_type=F32) + b_out
    resid = inputs + branch_a
    normed_b, unit_b, rstd_b = norm_rows(resid, gain_two, shift_two)
    hidden_b = normed_b.astype(BF16)

    logits = lax.dot_general(
        hidden_b, w_router_t, (((1,), (1,)), ((), ())), preferred_element_type=F32
    )
    one_hot = expert_ids[:, :, None] == jnp.arange(EXP, dtype=jnp.int32)[None, None, :]
    chosen = jnp.sum(jnp.where(one_hot, logits[:, None, :], 0.0), -1)
    chosen_max = jnp.max(chosen, -1, keepdims=True)
    chosen_exp = jnp.exp(chosen - chosen_max)
    gates = chosen_exp / jnp.sum(chosen_exp, -1, keepdims=True)
    blocks = to_experts(jnp.dot(spread, hidden_b, preferred_element_type=F32).astype(BF16))
    gate_cells = jnp.sum(
        jnp.where(hit_rows[0], gates[:, 0][None, :], 0.0)
        + jnp.where(hit_rows[1], gates[:, 1][None, :], 0.0),
        1,
    )
    gate_blocks = to_experts(gate_cells.reshape(EXP * CELLS // 128, 128).reshape(EXP * CELLS))
    inner = jnp.dot(blocks, w_in, preferred_element_type=F32) + b_in
    activ = smooth_gelu(inner).astype(BF16)
    expert_y = (jnp.dot(activ, w_exit, preferred_element_type=F32) + b_exit).astype(BF16)

    exit_grad = (gate_blocks[:, None] * cot_blocks.astype(F32)).astype(BF16)
    b_exit_grad = jnp.sum(exit_grad, 0, dtype=F32)
    activ_grad = lax.dot_general(
        exit_grad, w_exit, (((1,), (1,)), ((), ())), preferred_element_type=F32
    )
    inner_grad = jax.vjp(smooth_gelu, inner)[1](activ_grad)[0].astype(BF16)
    b_in_grad = jnp.sum(inner_grad, 0, dtype=F32)
    block_grad = lax.dot_general(
        inner_grad, w_in, (((1,), (1,)), ((), ())), preferred_element_type=F32
    ).astype(BF16)
    w_exit_grad = lax.dot_general(
        activ, exit_grad, (((0,), (0,)), ((), ())), preferred_element_type=F32
    ).astype(BF16)
    w_in_grad = lax.dot_general(
        blocks, inner_grad, (((0,), (0,)), ((), ())), preferred_element_type=F32
    ).astype(BF16)
    y_cells = to_experts(expert_y)
    grad_cells = to_experts(block_grad)
    w_in_sum = expert_scatter(w_in_grad, n, me, expert, x_first[::-1])
    w_exit_sum = expert_scatter(w_exit_grad, n, me, expert, y_first[::-1])

    grad_out = cotangent.astype(F32)
    picked = [
        lax.dot_general(
            hit_rows[k].astype(BF16), y_cells, (((0,), (0,)), ((), ())), preferred_element_type=F32
        )
        for k in range(2)
    ]
    mixed_out = (resid + (gates[:, :1] * picked[0] + gates[:, 1:] * picked[1])).astype(BF16)
    gate_grad = jnp.stack([jnp.sum(picked[k] * grad_out, -1) for k in range(2)], -1)
    hidden_b_grad = lax.dot_general(
        spread, grad_cells, (((0,), (0,)), ((), ())), preferred_element_type=F32
    )
    chosen_grad = gates * (gate_grad - jnp.sum(gates * gate_grad, -1, keepdims=True))
    logit_grad = jnp.sum(jnp.where(one_hot, chosen_grad[:, :, None], 0.0), 1).astype(BF16)
    router_grad_t = lax.dot_general(
        logit_grad, hidden_b, (((0,), (0,)), ((), ())), preferred_element_type=F32
    )
    hidden_b_grad = hidden_b_grad + jnp.dot(logit_grad, w_router_t, preferred_element_type=F32)
    resid_part, gain_two_grad, shift_two_grad = norm_back(hidden_b_grad, unit_b, rstd_b, gain_two)
    resid_grad = grad_out + resid_part
    branch_grad = resid_grad.astype(BF16)
    b_out_grad = jnp.sum(branch_grad, 0, dtype=F32)
    w_out_grad = jnp.einsum("td,te->de", attended, branch_grad, preferred_element_type=F32)
    attended_grad = (
        jnp.einsum("te,de->td", branch_grad, w_out, preferred_element_type=F32)
        .astype(BF16)
        .reshape(heads_shape)
    )
    scores_again = jnp.einsum("ishd,ithd->ihst", query_h, key_h, preferred_element_type=F32) * SCALE
    probs_again = jnp.exp(scores_again - log_total)
    value_grad = (
        jnp.einsum(
            "ihst,ishd->ithd", probs_again.astype(BF16), attended_grad, preferred_element_type=F32
        )
        .astype(BF16)
        .reshape(tok_rows, D)
    )
    prob_grad = jnp.einsum("ishd,ithd->ihst", attended_grad, value_h, preferred_element_type=F32)
    score_grad = (
        probs_again * (prob_grad - jnp.sum(probs_again * prob_grad, -1, keepdims=True))
    ).astype(BF16)
    query_grad = (
        (jnp.einsum("ihst,ithd->ishd", score_grad, key_h, preferred_element_type=F32) * SCALE)
        .astype(BF16)
        .reshape(tok_rows, D)
    )
    key_grad = (
        (jnp.einsum("ihst,ishd->ithd", score_grad, query_h, preferred_element_type=F32) * SCALE)
        .astype(BF16)
        .reshape(tok_rows, D)
    )
    b_query_grad = jnp.sum(query_grad, 0, dtype=F32)
    b_value_grad = jnp.sum(value_grad, 0, dtype=F32)
    w_query_grad = jnp.einsum("td,te->de", hidden_a, query_grad, preferred_element_type=F32)
    w_key_grad = jnp.einsum("td,te->de", hidden_a, key_grad, preferred_element_type=F32)
    w_value_grad = jnp.einsum("td,te->de", hidden_a, value_grad, preferred_element_type=F32)
    hidden_a_grad = jnp.einsum("te,de->td", query_grad, w_query, preferred_element_type=F32)
    hidden_a_grad = hidden_a_grad + jnp.einsum(
        "te,de->td", key_grad, w_key, preferred_element_type=F32
    )
    hidden_a_grad = hidden_a_grad + jnp.einsum(
        "te,de->td", value_grad, w_value, preferred_element_type=F32
    )
    input_part, gain_one_grad, shift_one_grad = norm_back(hidden_a_grad, unit_a, rstd_a, gain_one)
    tokens_grad = resid_grad + input_part

    own_expert = (jnp.arange(EXP, dtype=jnp.int32) == expert)[:, None]
    vec_grad = jnp.concatenate(
        [
            jnp.stack(
                [
                    gain_one_grad,
                    shift_one_grad,
                    b_query_grad,
                    b_value_grad,
                    b_out_grad,
                    gain_two_grad,
                    shift_two_grad,
                ]
            ),
            router_grad_t,
            jnp.where(own_expert, b_exit_grad[None, :], 0.0),
        ],
        0,
    ).astype(BF16)
    vec_grad = vec_grad.reshape(15, n, rows).transpose(1, 0, 2).reshape(n, 15 * rows)
    in_grad = jnp.where(own_expert, b_in_grad[None, :], 0.0).astype(BF16)
    in_grad = in_grad.reshape(EXP, n, ff_rows).transpose(1, 0, 2).reshape(n, EXP * ff_rows)
    small_grad = jnp.pad(
        jnp.concatenate([vec_grad, in_grad], 1), ((0, 0), (0, D - n_small))
    ).reshape(n, 1, D)

    def by_owner(grad):
        return grad.astype(BF16).reshape(n, rows, D)

    back_bits = far_bits[::-1]
    sum_b = scatter_sum(
        jnp.concatenate([by_owner(w_value_grad), by_owner(w_out_grad), small_grad], 1),
        n,
        me,
        [0, 1, 2, 3] + back_bits,
    ).astype(F32)
    sum_a = scatter_sum(
        jnp.concatenate([by_owner(w_query_grad), by_owner(w_key_grad)], 1),
        n,
        me,
        [0, 2, 1, 3] + back_bits,
    ).astype(F32)
    small_sum = sum_b[2 * rows]
    vec_sum = small_sum[: 15 * rows].reshape(15, rows)
    b_in_sum = small_sum[15 * rows : n_small].reshape(EXP, ff_rows)
    return (
        mixed_out,
        tokens_grad,
        vec_sum[0],
        vec_sum[1],
        sum_a[:rows],
        vec_sum[2],
        sum_a[rows:],
        sum_b[:rows],
        vec_sum[3],
        sum_b[rows : 2 * rows],
        vec_sum[4],
        vec_sum[5],
        vec_sum[6],
        vec_sum[7:11].T,
        w_in_sum,
        b_in_sum,
        w_exit_sum,
        vec_sum[11:15],
    )


def solution(mesh):
    in_specs = (
        P("fsdp", None),
        P("fsdp", None),
        P("fsdp", None),
        P("fsdp", None),
        P("fsdp"),
        P("fsdp"),
        P("fsdp", None),
        P("fsdp"),
        P("fsdp", None),
        P("fsdp", None),
        P("fsdp"),
        P("fsdp", None),
        P("fsdp"),
        P("fsdp"),
        P("fsdp"),
        P("fsdp", None),
        P(None, "fsdp", None),
        P(None, "fsdp"),
        P(None, "fsdp", None),
        P(None, "fsdp"),
    )
    out_specs = (
        P("fsdp", None),
        P("fsdp", None),
        P("fsdp"),
        P("fsdp"),
        P("fsdp", None),
        P("fsdp"),
        P("fsdp", None),
        P("fsdp", None),
        P("fsdp"),
        P("fsdp", None),
        P("fsdp"),
        P("fsdp"),
        P("fsdp"),
        P("fsdp", None),
        P(None, "fsdp", None),
        P(None, "fsdp"),
        P(None, "fsdp", None),
        P(None, "fsdp"),
    )
    return jax.shard_map(
        functools.partial(per_device, mesh.shape["fsdp"]),
        mesh=mesh,
        in_specs=in_specs,
        out_specs=out_specs,
        check_vma=False,
    )
```

```python
import functools

import jax
import jax.numpy as jnp
from jax import lax
from jax.experimental import pallas as pl
from jax.experimental.pallas import tpu as pltpu
from jax.sharding import PartitionSpec as P

D = 768
HEADS = 12
HEAD_DIM = 64
EXP = 4
SEQ = 197
CAP = 246
CELLS = 256


EPSILON = 1e-05
SCALE = 0.125
F32 = jnp.float32
BF16 = jnp.bfloat16
AXIS = "fsdp"

GROUP_BITS = (0, 3)


def group_mask(k):
    return (k & 1) << GROUP_BITS[0] | (k >> 1) << GROUP_BITS[1]


def norm_rows(values, gain, shift):
    mean_row = jnp.mean(values, -1, keepdims=True)
    centred = values - mean_row
    rstd_row = lax.rsqrt(jnp.mean(centred * centred, -1, keepdims=True) + EPSILON)
    unit_rows = centred * rstd_row
    return (unit_rows * gain + shift, unit_rows, rstd_row)


def norm_back(grad_in, unit_rows, rstd_row, gain):
    scaled = grad_in * gain
    input_grad = rstd_row * (
        scaled
        - jnp.mean(scaled, -1, keepdims=True)
        - unit_rows * jnp.mean(scaled * unit_rows, -1, keepdims=True)
    )
    return (input_grad, jnp.sum(grad_in * unit_rows, 0), jnp.sum(grad_in, 0))


def smooth_gelu(inner):
    return 0.5 * inner * (1.0 + jnp.tanh(0.7978845608 * (inner + 0.044715 * inner * inner * inner)))


def swap(x, n, mask):
    return lax.ppermute(x, AXIS, [(i, i ^ mask) for i in range(n)])


def bit_of(me, bit):
    return (me >> bit) & 1


def gather_all(x, n, me, order):
    width = n.bit_length() - 1
    x = x.reshape((1,) * width + x.shape)
    for bit in order:
        axis = width - 1 - bit
        other = swap(x, n, 1 << bit)
        high = bit_of(me, bit) == 1
        x = jnp.concatenate([jnp.where(high, other, x), jnp.where(high, x, other)], axis)
    return x.reshape((n,) + x.shape[width:])


def halve(x, n, me, bit, axis):
    mine = bit_of(me, bit)
    send = lax.dynamic_index_in_dim(x, 1 - mine, axis, keepdims=True)
    keep = lax.dynamic_index_in_dim(x, mine, axis, keepdims=True)
    other = swap(send, n, 1 << bit)
    return (keep.astype(F32) + other.astype(F32)).astype(BF16)


def scatter_sum(x, n, me, order):
    width = n.bit_length() - 1
    tail = x.shape[1:]
    x = x.reshape((2,) * width + tail)
    for bit in order:
        x = halve(x, n, me, bit, width - 1 - bit)
    return x.reshape(tail)


def after(x, *others):
    for other in others:
        x = x + (other[(0,) * other.ndim] * 0).astype(x.dtype)
    return x


def group_exchange(parts, n, then=()):
    from_z = swap(jnp.stack([parts[2], parts[3]]), n, group_mask(2))
    from_c = swap(after(jnp.stack([parts[1], from_z[1]]), *then), n, group_mask(1))
    return [parts[0], from_c[0], from_z[0], from_c[1]]


CHUNK = 768
TILE = 256


def expert_kernel(labels, me_ref, *refs):
    n_pieces = len(labels)
    pieces = refs[:n_pieces]
    blocks, cot, gate, b_in, b_exit, y_out, block_grad, gate_dot, b_in_grad, b_exit_grad = refs[
        n_pieces : n_pieces + 10
    ]
    refs = refs[n_pieces + 10 :]
    n_grads = len(refs) - 10
    grads = refs[:n_grads]
    (
        w_in,
        w_exit,
        exit_grad,
        activ,
        inner_grad,
        y_sum,
        block_sum,
        load_sems,
        in_sems,
        out_sems,
    ) = refs[n_grads:]
    step = pl.program_id(0)
    steps = pl.num_programs(0)
    rows = blocks.shape[0]
    chunks = w_in.shape[1] // CHUNK

    def units(arrays, names):
        number = 0
        for array, labels_here in zip(arrays, names, strict=True):
            for i, mask in enumerate(labels_here):
                pair = 0 if mask is None else (me_ref[0] ^ mask) >> 1
                yield number, array.at[i], pair, array.shape[1] // (2 * chunks)
                number += 1

    def in_place(block, pair, count, at):
        start = pl.multiple_of(pair * count, count)
        columns = pl.ds(pl.multiple_of(at * CHUNK, CHUNK), CHUNK)
        row = pl.multiple_of(at * count, count)
        return block.at[pl.ds(row, count)], w_in.at[pl.ds(start, count), columns]

    def out_place(block, pair, count):
        start = pl.multiple_of(pair * count * chunks, count * chunks)
        return (
            block.at[pl.ds(count * chunks, count * chunks)],
            w_exit.at[pl.ds(start, count * chunks)],
        )

    def loads():
        found = []
        for number, block, pair, count in units(pieces, labels):
            for at in range(chunks):
                found.append(
                    pltpu.make_async_copy(
                        *in_place(block, pair, count, at), load_sems.at[at, number]
                    )
                )
            found.append(
                pltpu.make_async_copy(*out_place(block, pair, count), load_sems.at[chunks, number])
            )
        return found

    def in_stores(at):
        return [
            pltpu.make_async_copy(*in_place(block, pair, count, at)[::-1], in_sems.at[at, number])
            for number, block, pair, count in units(grads, GRAD_LABELS if n_pieces > 1 else labels)
        ]

    def out_stores():
        return [
            pltpu.make_async_copy(*out_place(block, pair, count)[::-1], out_sems.at[number])
            for number, block, pair, count in units(grads, GRAD_LABELS if n_pieces > 1 else labels)
        ]

    @pl.when(step == 0)
    def _():
        arriving = loads()
        for copy in arriving:
            copy.start()
        exit_grad[...] = (gate[...] * cot[...].astype(F32)).astype(BF16)
        b_exit_grad[...] = jnp.sum(exit_grad[...].astype(F32), 0, keepdims=True)
        y_sum[...] = jnp.zeros_like(y_sum)
        block_sum[...] = jnp.zeros_like(block_sum)
        for copy in arriving:
            copy.wait()

    columns = pl.ds(pl.multiple_of(step * CHUNK, CHUNK), CHUNK)
    b_in_grad[...] = jnp.zeros_like(b_in_grad)

    def tile(i, carry):
        at = pl.ds(pl.multiple_of(i * TILE, TILE), TILE)
        w_in_part = w_in[:, columns]
        w_exit_part = w_exit[columns, :]
        inner = jnp.dot(blocks[at, :], w_in_part, preferred_element_type=F32) + b_in[...]
        square = inner * inner
        curve = jnp.tanh(0.7978845608 * (inner + 0.044715 * square * inner))
        half = 0.5 * (1.0 + curve)
        activ_tile = (half * inner).astype(BF16)
        slope = half + 0.5 * inner * (1.0 - curve * curve) * (
            0.7978845608 + (0.7978845608 * 3.0 * 0.044715) * square
        )
        activ[at, :] = activ_tile
        y_sum[at, :] += jnp.dot(activ_tile, w_exit_part, preferred_element_type=F32)
        activ_grad = lax.dot_general(
            exit_grad[at, :], w_exit_part, (((1,), (1,)), ((), ())), preferred_element_type=F32
        )
        grad_tile = (activ_grad * slope).astype(BF16)
        inner_grad[at, :] = grad_tile
        b_in_grad[...] += jnp.sum(grad_tile.astype(F32), 0, keepdims=True)
        block_sum[at, :] += lax.dot_general(
            grad_tile, w_in_part, (((1,), (1,)), ((), ())), preferred_element_type=F32
        )
        return carry

    lax.fori_loop(0, rows // TILE, tile, 0)
    w_in[:, columns] = lax.dot_general(
        blocks[...], inner_grad[...], (((0,), (0,)), ((), ())), preferred_element_type=F32
    ).astype(BF16)
    for copy in in_stores(step):
        copy.start()
    w_exit[columns, :] = lax.dot_general(
        activ[...], exit_grad[...], (((0,), (0,)), ((), ())), preferred_element_type=F32
    ).astype(BF16)

    @pl.when(step == steps - 1)
    def _():
        for copy in out_stores():
            copy.start()
        whole_y = y_sum[...] + b_exit[...]
        y_out[...] = whole_y.astype(BF16)
        gate_dot[...] = jnp.sum(whole_y * cot[...].astype(F32), -1, keepdims=True)
        block_grad[...] = block_sum[...].astype(BF16)
        for at in range(chunks):
            for copy in in_stores(at):
                copy.wait()
        for copy in out_stores():
            copy.wait()


X, Y, Z, NEAR = 2, 4, 16, 1 << GROUP_BITS[1]
GRAD_LABELS = tuple(
    tuple(mask | part for mask in masks)
    for part, (one, two) in ((0, (Y, X)), (NEAR, (X, Y)))
    for masks in ((one | Z, one | two | Z), (one, one | two), (Z, two | Z), (0, two))
)


def run_expert(pieces, labels, me, blocks, cot, gate, b_in, b_exit):
    rows = blocks.shape[0]
    ff = b_in.shape[1]
    chunks = ff // CHUNK
    any_spec = pl.BlockSpec(memory_space=pl.ANY)
    n_units = sum(len(names) for names in labels)
    if len(pieces) > 1:
        grad_shapes = [(len(names),) + pieces[0].shape[1:] for names in GRAD_LABELS]
    else:
        grad_shapes = [pieces[0].shape]

    def whole(shape):
        return pl.BlockSpec(shape, lambda i: (0,) * len(shape))

    results = pl.pallas_call(
        functools.partial(expert_kernel, labels),
        grid=(chunks,),
        out_shape=[
            jax.ShapeDtypeStruct((rows, D), BF16),
            jax.ShapeDtypeStruct((rows, D), BF16),
            jax.ShapeDtypeStruct((rows, 1), F32),
            jax.ShapeDtypeStruct((1, ff), F32),
            jax.ShapeDtypeStruct((1, D), F32),
        ]
        + [jax.ShapeDtypeStruct(shape, BF16) for shape in grad_shapes],
        in_specs=[pl.BlockSpec(memory_space=pltpu.SMEM)]
        + [any_spec] * len(pieces)
        + [
            whole((rows, D)),
            whole((rows, D)),
            whole((rows, 1)),
            pl.BlockSpec((1, CHUNK), lambda i: (0, i)),
            whole((1, D)),
        ],
        out_specs=[
            whole((rows, D)),
            whole((rows, D)),
            whole((rows, 1)),
            pl.BlockSpec((1, CHUNK), lambda i: (0, i)),
            whole((1, D)),
        ]
        + [any_spec] * len(grad_shapes),
        scratch_shapes=[
            pltpu.VMEM((D, ff), BF16),
            pltpu.VMEM((ff, D), BF16),
            pltpu.VMEM((rows, D), BF16),
            pltpu.VMEM((rows, CHUNK), BF16),
            pltpu.VMEM((rows, CHUNK), BF16),
            pltpu.VMEM((rows, D), F32),
            pltpu.VMEM((rows, D), F32),
            pltpu.SemaphoreType.DMA((chunks + 1, n_units)),
            pltpu.SemaphoreType.DMA((chunks, n_units)),
            pltpu.SemaphoreType.DMA((n_units,)),
        ],
        compiler_params=pltpu.CompilerParams(
            vmem_limit_bytes=58 * 2**20, dimension_semantics=("arbitrary",)
        ),
    )(me.reshape(1).astype(jnp.int32), *pieces, blocks, cot, gate, b_in, b_exit)
    return results[:5], results[5:]


def expert_gather(shards, n, me):
    parts = group_exchange(shards, n)
    high = bit_of(me, GROUP_BITS[0]) == 1
    rows = shards[0].shape[0] // 8

    def pair(first, second):
        def part(low, count):
            here, there = first[low : low + count], second[low : low + count]
            here = here.reshape(-1, 1, count // 4 if low == 0 else count, D)
            there = there.reshape(here.shape)
            return jnp.concatenate(
                [jnp.where(high, there, here), jnp.where(high, here, there)], 1
            ).reshape(2 * count, D)

        return jnp.concatenate([part(0, 4 * rows), part(4 * rows, 4 * rows)])[None]

    halves = (pair(parts[0], parts[1]), pair(parts[2], parts[3]))
    if n != 32:
        return halves
    far = [swap(half, n, Z) for half in halves]
    first = [swap(half, n, one) for half, one in zip(halves, (X, Y))]
    return halves, first, far


def expert_gather_rest(sent, n, me, wait_own, wait_far):
    if n == 32:
        pieces, labels = [], []
        halves, first, far = sent
        for half, got, part, one in zip(halves, first, (0, NEAR), (X, Y)):
            two = X ^ Y ^ one
            both = swap(after(jnp.concatenate([half, got]), *wait_own), n, two)
            pieces += [half, got, both]
            labels += [(part,), (part | one,), (part | two, part | one | two)]
        far = [after(half, *wait_far) for half in far]
        first = [swap(half, n, one) for half, one in zip(far, (X, Y))]
        for half, got, part, one in zip(far, first, (0, NEAR), (X, Y)):
            two = X ^ Y ^ one
            both = swap(jnp.concatenate([half, got]), n, two)
            pieces += [half, got, both]
            labels += [(part | Z,), (part | one | Z,), (part | two | Z, part | one | two | Z)]
        return pieces, tuple(labels)
    by_mask = {0: sent[0], NEAR: sent[1]}
    for bit in range(n.bit_length() - 1):
        if bit not in GROUP_BITS:
            for mask in list(by_mask):
                by_mask[mask | 1 << bit] = swap(by_mask[mask], n, 1 << bit)
    order = (jnp.arange(n // 2, dtype=jnp.int32) ^ (me >> 1))
    blocks = jnp.take(
        jnp.concatenate([by_mask[2 * pair] for pair in range(n // 2)]), order, axis=0
    )
    rows = blocks.shape[1] // 16
    w_in = blocks[:, : 8 * rows].reshape(n // 2, 4, 2 * rows, D)
    w_in = w_in.transpose(1, 0, 2, 3).reshape(4 * n * rows, D)
    return [jnp.concatenate([w_in, blocks[:, 8 * rows :].reshape(-1, D)])[None]], ((None,),)


def add(*terms):
    total = terms[0].astype(F32)
    for term in terms[1:]:
        total = total + term.astype(F32)
    return total.astype(BF16)


def expert_scatter(grads, n, me, wait_two, wait_three, wait_last):
    if n == 32:
        firsts = []
        for at, one in ((0, Y), (4, X)):
            firsts.append(swap(grads[at], n, one))
        seconds = []
        for at, one in ((0, Y), (4, X)):
            two = X ^ Y ^ one
            got = firsts[at // 4]
            across = swap(after(add(grads[at + 2][1], got[1]), *wait_two), n, two)
            seconds.append((swap(grads[at + 1], n, one), across))
        sums = []
        for at, one in ((0, Y), (4, X)):
            two = X ^ Y ^ one
            got, across = seconds[at // 4]
            far = add(grads[at + 2][0], firsts[at // 4][0], across)
            near = swap(after(add(grads[at + 3][1], got[1]), *wait_three), n, two)
            far = swap(after(far, *wait_three), n, Z)
            sums.append(after(add(grads[at + 3][0], got[0], near, far), *wait_last))
    else:
        whole = grads[0][0]
        rows = whole.shape[0] // (8 * n)
        half = whole.shape[0] // 2
        w_in = whole[:half].reshape(4, n // 2, 2 * rows, D).transpose(1, 0, 2, 3)
        w_in = w_in.reshape(n // 2, 8 * rows, D)
        x = jnp.concatenate([w_in, whole[half:].reshape(n // 2, 8 * rows, D)], 1)
        width = n.bit_length() - 1
        x = x.reshape((2,) * (width - 1) + (16 * rows, D))
        for bit in range(1, width):
            if bit not in GROUP_BITS:
                x = halve(x, n, me, bit, width - 1 - bit)
        x = x.reshape(2, 16 * rows, D)
        near = bit_of(me, GROUP_BITS[1])
        sums = [lax.dynamic_index_in_dim(x, near ^ k, 0, keepdims=False) for k in range(2)]
    high = bit_of(me, GROUP_BITS[0]) == 1
    half = sums[0].shape[0] // 2

    def side(total, k):
        w_in = total[:half].reshape(4, 2, half // 8, D)
        w_exit = total[half:].reshape(2, half // 2, D)
        return jnp.concatenate(
            [
                jnp.where(high, w_in[:, 1 - k], w_in[:, k]).reshape(half // 2, D),
                jnp.where(high, w_exit[1 - k], w_exit[k]),
            ]
        )

    return group_exchange([side(sums[k >> 1], k & 1) for k in range(EXP)], n)


def per_device(
    n,
    tokens,
    cotangent,
    expert_ids,
    slots,
    norm1_gain,
    norm1_shift,
    query_weight,
    query_bias,
    key_weight,
    value_weight,
    value_bias,
    out_weight,
    out_bias,
    norm2_gain,
    norm2_shift,
    router_weight,
    expert_in,
    expert_in_bias,
    expert_out,
    expert_out_bias,
):
    me = lax.axis_index(AXIS)
    width = n.bit_length() - 1
    expert = bit_of(me, GROUP_BITS[0]) | bit_of(me, GROUP_BITS[1]) << 1
    far_bits = [b for b in range(width) if b not in GROUP_BITS and b > 2][::-1]
    rows = query_weight.shape[0]
    ff_rows = expert_out.shape[1]
    ff = ff_rows * n
    tok_rows = tokens.shape[0]
    images = tok_rows // SEQ
    heads_shape = (images, SEQ, HEADS, HEAD_DIM)

    vectors = jnp.stack(
        [norm1_gain, norm1_shift, query_bias, value_bias, out_bias, norm2_gain, norm2_shift]
    )
    small = jnp.concatenate(
        [vectors, router_weight.T, expert_out_bias], 0
    ).reshape(-1)
    small = jnp.concatenate([small, expert_in_bias.reshape(-1)])
    n_small = small.shape[0]
    small = jnp.pad(small, (0, D - n_small)).reshape(1, D)
    pack_a = jnp.concatenate([query_weight, key_weight], 0)
    pack_b = jnp.concatenate([value_weight, out_weight, small], 0)
    full_a = gather_all(pack_a, n, me, far_bits + [3, 1, 2, 0])
    full_b = gather_all(pack_b, n, me, far_bits + [3, 2, 1, 0])
    w_query = full_a[:, :rows].reshape(D, D)
    w_key = full_a[:, rows:].reshape(D, D)
    w_value = full_b[:, :rows].reshape(D, D)
    w_out = full_b[:, rows : 2 * rows].reshape(D, D)
    small_full = full_b[:, 2 * rows]
    vec = small_full[:, : 15 * rows].reshape(n, 15, rows).transpose(1, 0, 2).reshape(15, D)
    gain_one, shift_one, b_query, b_value, b_out, gain_two, shift_two = [
        vec[i].astype(F32) for i in range(7)
    ]
    w_router_t = vec[7:11]
    b_exit = lax.dynamic_index_in_dim(vec[11:15], expert, 0, keepdims=True).astype(F32)
    b_in_all = small_full[:, 15 * rows : n_small].reshape(n, EXP, ff_rows)
    b_in = lax.dynamic_index_in_dim(b_in_all, expert, 1, keepdims=False).reshape(1, ff).astype(F32)

    in_chunks = expert_in.reshape(EXP, rows, 4, D).transpose(0, 2, 1, 3).reshape(EXP, 4 * rows, D)
    shards = jnp.concatenate([in_chunks, expert_out], 1)
    shards = [
        lax.dynamic_index_in_dim(shards, expert ^ k, 0, keepdims=False) for k in range(EXP)
    ]
    sent = expert_gather(shards, n, me)

    cell_index = (expert_ids ^ expert) * CELLS + slots
    cell_ids = jnp.arange(EXP * CELLS, dtype=jnp.int32)
    hit_rows = [
        (cell_index[:, k][None, :] == cell_ids[:, None]) for k in range(2)
    ]
    spread = (hit_rows[0] | hit_rows[1]).astype(BF16)
    cot_cells = jnp.dot(spread, cotangent, preferred_element_type=F32).astype(BF16)

    def to_experts(cells, then=()):
        return jnp.concatenate(
            group_exchange(cells.reshape((EXP, CELLS) + cells.shape[1:]), n, then), 0
        )

    inputs = tokens.astype(F32)
    normed_a, unit_a, rstd_a = norm_rows(inputs, gain_one, shift_one)
    hidden_a = normed_a.astype(BF16)
    query = (jnp.dot(hidden_a, w_query, preferred_element_type=F32) + b_query).astype(BF16)
    keys_all = jnp.dot(hidden_a, w_key, preferred_element_type=F32).astype(BF16)
    values_all = (jnp.dot(hidden_a, w_value, preferred_element_type=F32) + b_value).astype(BF16)
    cot_blocks = to_experts(after(cot_cells, full_a, full_b), (query, values_all))
    query_h = query.reshape(heads_shape)
    key_h = keys_all.reshape(heads_shape)
    value_h = values_all.reshape(heads_shape)
    scores = jnp.einsum("ishd,ithd->ihst", query_h, key_h, preferred_element_type=F32) * SCALE
    row_max = jnp.max(scores, -1, keepdims=True)
    raised = jnp.exp(scores - row_max)
    row_total = jnp.sum(raised, -1, keepdims=True)
    probs = raised / row_total
    log_total = row_max + jnp.log(row_total)
    mixed_h = jnp.einsum("ihst,ithd->ishd", probs.astype(BF16), value_h, preferred_element_type=F32)
    attended = mixed_h.astype(BF16).reshape(tok_rows, D)
    branch_a = jnp.dot(attended, w_out, preferred_element_type=F32) + b_out
    resid = inputs + branch_a
    normed_b, unit_b, rstd_b = norm_rows(resid, gain_two, shift_two)
    hidden_b = normed_b.astype(BF16)

    pieces, labels = expert_gather_rest(
        sent, n, me, (query, keys_all, values_all), (attended, cot_blocks)
    )

    logits = lax.dot_general(
        hidden_b, w_router_t, (((1,), (1,)), ((), ())), preferred_element_type=F32
    )
    one_hot = expert_ids[:, :, None] == jnp.arange(EXP, dtype=jnp.int32)[None, None, :]
    chosen = jnp.sum(jnp.where(one_hot, logits[:, None, :], 0.0), -1)
    chosen_max = jnp.max(chosen, -1, keepdims=True)
    chosen_exp = jnp.exp(chosen - chosen_max)
    gates = chosen_exp / jnp.sum(chosen_exp, -1, keepdims=True)
    blocks = to_experts(jnp.dot(spread, hidden_b, preferred_element_type=F32).astype(BF16))
    gate_cells = jnp.sum(
        jnp.where(hit_rows[0], gates[:, 0][None, :], 0.0)
        + jnp.where(hit_rows[1], gates[:, 1][None, :], 0.0),
        1,
    )
    gate_blocks = to_experts(gate_cells)
    (expert_y, block_grad, gate_dot, b_in_grad, b_exit_grad), w_grads = run_expert(
        pieces, labels, me, blocks, cot_blocks, gate_blocks.reshape(-1, 1), b_in, b_exit
    )
    dot_cells = to_experts(gate_dot.reshape(-1))
    grad_cells = to_experts(block_grad)
    grad_out = cotangent.astype(F32)
    gate_grad = jnp.stack(
        [jnp.sum(jnp.where(hit_rows[k], dot_cells[:, None], 0.0), 0) for k in range(2)], -1
    )
    hidden_b_grad = lax.dot_general(
        spread, grad_cells, (((0,), (0,)), ((), ())), preferred_element_type=F32
    )
    chosen_grad = gates * (gate_grad - jnp.sum(gates * gate_grad, -1, keepdims=True))
    logit_grad = jnp.sum(jnp.where(one_hot, chosen_grad[:, :, None], 0.0), 1).astype(BF16)
    router_grad_t = lax.dot_general(
        logit_grad, hidden_b, (((0,), (0,)), ((), ())), preferred_element_type=F32
    )
    hidden_b_grad = hidden_b_grad + jnp.dot(logit_grad, w_router_t, preferred_element_type=F32)
    resid_part, gain_two_grad, shift_two_grad = norm_back(hidden_b_grad, unit_b, rstd_b, gain_two)
    resid_grad = grad_out + resid_part
    branch_grad = resid_grad.astype(BF16)
    b_out_grad = jnp.sum(branch_grad, 0, dtype=F32)
    w_out_grad = jnp.einsum("td,te->de", attended, branch_grad, preferred_element_type=F32)
    y_cells = to_experts(after(expert_y, grad_cells), (branch_grad,))
    attended_grad = (
        jnp.einsum("te,de->td", branch_grad, w_out, preferred_element_type=F32)
        .astype(BF16)
        .reshape(heads_shape)
    )
    scores_again = jnp.einsum("ishd,ithd->ihst", query_h, key_h, preferred_element_type=F32) * SCALE
    probs_again = jnp.exp(scores_again - log_total)
    value_grad = (
        jnp.einsum(
            "ihst,ishd->ithd", probs_again.astype(BF16), attended_grad, preferred_element_type=F32
        )
        .astype(BF16)
        .reshape(tok_rows, D)
    )
    prob_grad = jnp.einsum("ishd,ithd->ihst", attended_grad, value_h, preferred_element_type=F32)
    score_grad = (
        probs_again * (prob_grad - jnp.sum(probs_again * prob_grad, -1, keepdims=True))
    ).astype(BF16)
    query_grad = (
        (jnp.einsum("ihst,ithd->ishd", score_grad, key_h, preferred_element_type=F32) * SCALE)
        .astype(BF16)
        .reshape(tok_rows, D)
    )
    key_grad = (
        (jnp.einsum("ihst,ishd->ithd", score_grad, query_h, preferred_element_type=F32) * SCALE)
        .astype(BF16)
        .reshape(tok_rows, D)
    )
    b_query_grad = jnp.sum(query_grad, 0, dtype=F32)
    b_value_grad = jnp.sum(value_grad, 0, dtype=F32)
    w_query_grad = jnp.einsum("td,te->de", hidden_a, query_grad, preferred_element_type=F32)
    w_key_grad = jnp.einsum("td,te->de", hidden_a, key_grad, preferred_element_type=F32)
    w_value_grad = jnp.einsum("td,te->de", hidden_a, value_grad, preferred_element_type=F32)
    hidden_a_grad = jnp.einsum("te,de->td", query_grad, w_query, preferred_element_type=F32)
    hidden_a_grad = hidden_a_grad + jnp.einsum(
        "te,de->td", key_grad, w_key, preferred_element_type=F32
    )
    hidden_a_grad = hidden_a_grad + jnp.einsum(
        "te,de->td", value_grad, w_value, preferred_element_type=F32
    )
    input_part, gain_one_grad, shift_one_grad = norm_back(hidden_a_grad, unit_a, rstd_a, gain_one)
    tokens_grad = resid_grad + input_part

    picked = [
        lax.dot_general(
            hit_rows[k].astype(BF16), y_cells, (((0,), (0,)), ((), ())), preferred_element_type=F32
        )
        for k in range(2)
    ]
    mixed_out = (resid + (gates[:, :1] * picked[0] + gates[:, 1:] * picked[1])).astype(BF16)

    w_sums = expert_scatter(
        w_grads, n, me, (branch_grad,), (value_grad,), (query_grad, key_grad)
    )
    places = jnp.arange(EXP, dtype=jnp.int32) ^ expert
    w_sums = jnp.stack([lax.select_n(places[i], *w_sums) for i in range(EXP)]).astype(F32)
    w_in_sum = w_sums[:, : 4 * rows].reshape(EXP, 4, rows, D).transpose(0, 2, 1, 3)
    w_in_sum = w_in_sum.reshape(EXP, rows, ff)
    w_exit_sum = w_sums[:, 4 * rows :]

    own_expert = (jnp.arange(EXP, dtype=jnp.int32) == expert)[:, None]
    vec_grad = jnp.concatenate(
        [
            jnp.stack(
                [
                    gain_one_grad,
                    shift_one_grad,
                    b_query_grad,
                    b_value_grad,
                    b_out_grad,
                    gain_two_grad,
                    shift_two_grad,
                ]
            ),
            router_grad_t,
            jnp.where(own_expert, b_exit_grad, 0.0),
        ],
        0,
    ).astype(BF16)
    vec_grad = vec_grad.reshape(15, n, rows).transpose(1, 0, 2).reshape(n, 15 * rows)
    in_grad = jnp.where(own_expert, b_in_grad, 0.0).astype(BF16)
    in_grad = in_grad.reshape(EXP, n, ff_rows).transpose(1, 0, 2).reshape(n, EXP * ff_rows)
    small_grad = jnp.pad(
        jnp.concatenate([vec_grad, in_grad], 1), ((0, 0), (0, D - n_small))
    ).reshape(n, 1, D)

    def by_owner(grad):
        return grad.astype(BF16).reshape(n, rows, D)

    back_bits = [3] + far_bits[::-1]
    sum_b = scatter_sum(
        jnp.concatenate([by_owner(w_out_grad), by_owner(w_value_grad)], 1),
        n,
        me,
        [0, 1, 2] + back_bits,
    ).astype(F32)
    sum_a = scatter_sum(by_owner(w_query_grad), n, me, [0, 2, 1] + back_bits).astype(F32)
    sum_c = scatter_sum(
        jnp.concatenate([by_owner(w_key_grad), small_grad], 1), n, me, [0, 1, 2] + back_bits
    ).astype(F32)
    small_sum = sum_c[rows]
    vec_sum = small_sum[: 15 * rows].reshape(15, rows)
    b_in_sum = small_sum[15 * rows : n_small].reshape(EXP, ff_rows)
    return (
        mixed_out,
        tokens_grad,
        vec_sum[0],
        vec_sum[1],
        sum_a,
        vec_sum[2],
        sum_c[:rows],
        sum_b[rows:],
        vec_sum[3],
        sum_b[:rows],
        vec_sum[4],
        vec_sum[5],
        vec_sum[6],
        vec_sum[7:11].T,
        w_in_sum,
        b_in_sum,
        w_exit_sum,
        vec_sum[11:15],
    )


def solution(mesh):
    in_specs = (
        P("fsdp", None),
        P("fsdp", None),
        P("fsdp", None),
        P("fsdp", None),
        P("fsdp"),
        P("fsdp"),
        P("fsdp", None),
        P("fsdp"),
        P("fsdp", None),
        P("fsdp", None),
        P("fsdp"),
        P("fsdp", None),
        P("fsdp"),
        P("fsdp"),
        P("fsdp"),
        P("fsdp", None),
        P(None, "fsdp", None),
        P(None, "fsdp"),
        P(None, "fsdp", None),
        P(None, "fsdp"),
    )
    out_specs = (
        P("fsdp", None),
        P("fsdp", None),
        P("fsdp"),
        P("fsdp"),
        P("fsdp", None),
        P("fsdp"),
        P("fsdp", None),
        P("fsdp", None),
        P("fsdp"),
        P("fsdp", None),
        P("fsdp"),
        P("fsdp"),
        P("fsdp"),
        P("fsdp", None),
        P(None, "fsdp", None),
        P(None, "fsdp"),
        P(None, "fsdp", None),
        P(None, "fsdp"),
    )
    return jax.shard_map(
        functools.partial(per_device, mesh.shape["fsdp"]),
        mesh=mesh,
        in_specs=in_specs,
        out_specs=out_specs,
        check_vma=False,
    )
```

```python
import functools

import jax
import jax.numpy as jnp
from jax import lax
from jax.experimental import pallas as pl
from jax.experimental.pallas import tpu as pltpu
from jax.sharding import PartitionSpec as P

D = 768
HEADS = 12
HEAD_DIM = 64
EXP = 4
SEQ = 197
CAP = 246
CELLS = 256
ROWS = 208
LANES = 128


EPSILON = 1e-05
SCALE = 0.125
F32 = jnp.float32
BF16 = jnp.bfloat16
AXIS = "fsdp"

GROUP_BITS = (0, 3)


def group_mask(k):
    return (k & 1) << GROUP_BITS[0] | (k >> 1) << GROUP_BITS[1]


def swap(x, n, mask):
    return lax.ppermute(x, AXIS, [(i, i ^ mask) for i in range(n)])


def bit_of(me, bit):
    return (me >> bit) & 1


def gather_step(x, n, me, bit):
    axis = n.bit_length() - 2 - bit
    other = swap(x, n, 1 << bit)
    high = bit_of(me, bit) == 1
    return jnp.concatenate([jnp.where(high, other, x), jnp.where(high, x, other)], axis)


def halve(x, n, me, bit, axis):
    mine = bit_of(me, bit)
    send = lax.dynamic_index_in_dim(x, 1 - mine, axis, keepdims=True)
    keep = lax.dynamic_index_in_dim(x, mine, axis, keepdims=True)
    other = swap(send, n, 1 << bit)
    return (keep.astype(F32) + other.astype(F32)).astype(BF16)


def split_owners(x, n):
    return x.reshape((2,) * (n.bit_length() - 1) + x.shape[1:])


def sum_step(arrays, n, me, bits):
    width = n.bit_length() - 1
    sent, kept = [], []
    for x in arrays:
        for mask in range(1 << len(bits)):
            starts, sizes = [0] * x.ndim, list(x.shape)
            whole = 0
            for i, bit in enumerate(bits):
                axis = width - 1 - bit
                flip = mask >> i & 1
                starts[axis], sizes[axis] = bit_of(me, bit) ^ flip, 1
                whole |= flip << bit
            part = lax.dynamic_slice(x, starts, sizes)
            if mask:
                sent.append(swap(part, n, whole))
            else:
                kept.append(part.astype(F32))
    each = (1 << len(bits)) - 1
    found = []
    for i, total in enumerate(kept):
        for other in sent[i * each : (i + 1) * each]:
            total = total + other.astype(F32)
        found.append(total.astype(BF16))
    return found


def call(kernel, outs, ins, passed=(), others=()):
    n_ins, n_passed = len(ins), len(passed)

    def body(*refs):
        at = n_ins + n_passed + len(others)
        kernel(*refs[:n_ins], *refs[at : at + len(outs)])

    any_spec = pl.BlockSpec(memory_space=pl.ANY)
    vmem = pl.BlockSpec(memory_space=pltpu.VMEM)
    found = pl.pallas_call(
        body,
        out_shape=[jax.ShapeDtypeStruct(*out) for out in outs]
        + [jax.ShapeDtypeStruct(x.shape, x.dtype) for x in passed],
        in_specs=[vmem] * n_ins + [any_spec] * (n_passed + len(others)),
        out_specs=[vmem] * len(outs) + [any_spec] * n_passed,
        input_output_aliases={n_ins + i: len(outs) + i for i in range(n_passed)},
        compiler_params=pltpu.CompilerParams(vmem_limit_bytes=56 * 2**20),
    )(*ins, *passed, *others)
    return (*found[: len(outs)], list(found[len(outs) :]))


def gate(values, *others):
    return call(lambda *refs: None, [], [], values, others)[0]


def dot(a, b):
    return jnp.dot(a, b, preferred_element_type=F32)


def dot_nt(a, b):
    return lax.dot_general(a, b, (((1,), (1,)), ((), ())), preferred_element_type=F32)


def dot_tn(a, b):
    return lax.dot_general(a, b, (((0,), (0,)), ((), ())), preferred_element_type=F32)


def unit_rows(values):
    centred = values - jnp.mean(values, -1, keepdims=True)
    rstd = lax.rsqrt(jnp.mean(centred * centred, -1, keepdims=True) + EPSILON)
    return centred * rstd, rstd


def norm_back(grad, unit, rstd, gain):
    scaled = grad * gain
    return rstd * (
        scaled
        - jnp.mean(scaled, -1, keepdims=True)
        - unit * jnp.mean(scaled * unit, -1, keepdims=True)
    )


GAIN_ONE, SHIFT_ONE, B_QUERY, B_VALUE, B_OUT, GAIN_TWO, SHIFT_TWO = range(7)


def row_of(vec, i):
    return vec[i : i + 1, :]


def project_kernel(tok, vec, w_query, w_key, w_value, hidden, query, keys, values):
    unit, _ = unit_rows(tok[...].astype(F32))
    normed = (unit * row_of(vec, GAIN_ONE) + row_of(vec, SHIFT_ONE)).astype(BF16)
    hidden[...] = normed
    query[...] = (dot(normed, w_query[...]) + row_of(vec, B_QUERY)).astype(BF16)
    keys[...] = dot(normed, w_key[...]).astype(BF16)
    values[...] = (dot(normed, w_value[...]) + row_of(vec, B_VALUE)).astype(BF16)


def head_masks():
    lane = lax.broadcasted_iota(jnp.int32, (ROWS, LANES), 1)
    return [jnp.where(lane // HEAD_DIM == h, 1.0, 0.0).astype(BF16) for h in range(2)]


def head_probs(query, keys):
    scores = dot_nt(query, keys) * SCALE
    lane = lax.broadcasted_iota(jnp.int32, scores.shape, 1)
    scores = jnp.where(lane < SEQ, scores, -1e30)
    raised = jnp.exp(scores - jnp.max(scores, -1, keepdims=True))
    return raised * (1.0 / jnp.sum(raised, -1, keepdims=True))


def lane_hits(cell_cols, k):
    lane = lax.broadcasted_iota(jnp.int32, (cell_cols.shape[0], EXP * CELLS), 1)
    return lane == cell_cols[:, k : k + 1]


def attend_kernel(
    query,
    keys,
    values,
    tok,
    vec,
    w_out,
    w_router,
    id_cols,
    cell_cols,
    attended,
    resid,
    hidden,
    gates,
    cells,
):
    masks = head_masks()

    def image(i, carry):
        rows = pl.ds(pl.multiple_of(i * ROWS, ROWS), ROWS)
        for pair in range(HEADS // 2):
            lanes = pl.ds(pair * LANES, LANES)
            q, k, v = query[rows, lanes], keys[rows, lanes], values[rows, lanes]
            total = None
            for mask in masks:
                probs = head_probs(q * mask, k).astype(BF16)
                part = dot(probs, v * mask)
                total = part if total is None else total + part
            attended[rows, lanes] = total.astype(BF16)
        return carry

    lax.fori_loop(0, tok.shape[0] // ROWS, image, 0)
    total = tok[...].astype(F32) + (dot(attended[...], w_out[...]) + row_of(vec, B_OUT))
    resid[...] = total
    unit, _ = unit_rows(total)
    normed = (unit * row_of(vec, GAIN_TWO) + row_of(vec, SHIFT_TWO)).astype(BF16)
    hidden[...] = normed
    logits = dot_nt(normed, w_router[...])
    lane = lax.broadcasted_iota(jnp.int32, logits.shape, 1)
    chosen = [
        jnp.sum(jnp.where(lane == id_cols[:, k : k + 1], logits, 0.0), -1, keepdims=True)
        for k in range(2)
    ]
    most = jnp.maximum(chosen[0], chosen[1])
    raised = [jnp.exp(one - most) for one in chosen]
    both = raised[0] + raised[1]
    shares = [one / both for one in raised]
    gates[...] = jnp.where(lane == 0, shares[0], jnp.where(lane == 1, shares[1], 0.0))
    hits = [lane_hits(cell_cols, k) for k in range(2)]
    spread = jnp.where(hits[0] | hits[1], 1.0, 0.0).astype(BF16)
    cells[...] = dot_tn(spread, normed).astype(BF16)
    notes = None
    for hit, share in zip(hits, shares):
        thirds = jnp.zeros(logits.shape, F32)
        for third in range(3):
            part = share.astype(BF16).astype(F32)
            thirds = jnp.where(lane == third, part, thirds)
            share = share - part
        found = dot_tn(thirds.astype(BF16), jnp.where(hit, 1.0, 0.0).astype(BF16))
        notes = found if notes is None else notes + found
    write_notes(cells, notes)


def write_notes(cells, notes):
    first = CAP // 16 * 16
    row = lax.broadcasted_iota(jnp.int32, (CELLS - first, CELLS), 0) + first
    for member in range(EXP):
        found = jnp.zeros((CELLS - first, CELLS), F32)
        for third in range(3):
            note = notes[third : third + 1, member * CELLS : (member + 1) * CELLS]
            found = jnp.where(row == CAP + third, note, found)
        at = pl.ds(member * CELLS + first, CELLS - first)
        cells[at, :CELLS] = (cells[at, :CELLS].astype(F32) + found).astype(BF16)


def read_notes(cells):
    first = CAP // 16 * 16
    row = lax.broadcasted_iota(jnp.int32, (CELLS - first, CELLS), 0) + first
    mine = (row >= CAP) & (row < CAP + 3)
    found = []
    for member in range(EXP):
        at = pl.ds(member * CELLS + first, CELLS - first)
        block = cells[at, :CELLS].astype(F32)
        found.append(jnp.sum(jnp.where(mine, block, 0.0), 0, keepdims=True))
    return jnp.concatenate(found, 1)


def branch_back_kernel(
    grad_cells,
    id_cols,
    cell_cols,
    gates,
    hidden,
    attended,
    resid,
    cot,
    vec,
    w_router,
    w_out,
    resid_grad,
    attended_grad,
    w_out_grad,
    router_grad,
    sums,
):
    dots = read_notes(grad_cells)
    hits = [lane_hits(cell_cols, k) for k in range(2)]
    spread = jnp.where(hits[0] | hits[1], 1.0, 0.0).astype(BF16)
    gate_grad = [jnp.sum(jnp.where(hit, dots, 0.0), -1, keepdims=True) for hit in hits]
    shares = [gates[:, k : k + 1] for k in range(2)]
    mean = shares[0] * gate_grad[0] + shares[1] * gate_grad[1]
    lane = lax.broadcasted_iota(jnp.int32, gates.shape, 1)
    logit_grad = jnp.zeros(gates.shape, F32)
    for k in range(2):
        chosen_grad = shares[k] * (gate_grad[k] - mean)
        logit_grad += jnp.where(lane == id_cols[:, k : k + 1], chosen_grad, 0.0)
    logit_grad = logit_grad.astype(BF16)
    router_grad[...] = dot_tn(logit_grad, hidden[...])[:8]
    grad = dot(spread, grad_cells[...]) + dot(logit_grad, w_router[...])
    unit, rstd = unit_rows(resid[...])
    sums[0:1, :] = jnp.sum(grad * unit, 0, keepdims=True)
    sums[1:2, :] = jnp.sum(grad, 0, keepdims=True)
    total = cot[...].astype(F32) + norm_back(grad, unit, rstd, row_of(vec, GAIN_TWO))
    resid_grad[...] = total
    branch = total.astype(BF16)
    sums[2:3, :] = jnp.sum(branch.astype(F32), 0, keepdims=True)
    attended_grad[...] = dot_nt(branch, w_out[...]).astype(BF16)
    w_out_grad[...] = dot_tn(attended[...], branch).astype(BF16)


def attend_back_kernel(query, keys, values, attended_grad, query_grad, key_grad, value_grad):
    masks = head_masks()

    def image(i, carry):
        rows = pl.ds(pl.multiple_of(i * ROWS, ROWS), ROWS)
        for pair in range(HEADS // 2):
            lanes = pl.ds(pair * LANES, LANES)
            q, k, v = query[rows, lanes], keys[rows, lanes], values[rows, lanes]
            grad = attended_grad[rows, lanes]
            totals = None
            for mask in masks:
                own_q, own_grad = q * mask, grad * mask
                probs = head_probs(own_q, k)
                prob_grad = dot_nt(own_grad, v)
                mean = jnp.sum(probs * prob_grad, -1, keepdims=True)
                score_grad = (probs * (prob_grad - mean)).astype(BF16)
                parts = (
                    dot(score_grad, k * mask),
                    dot_tn(score_grad, own_q),
                    dot_tn(probs.astype(BF16), own_grad),
                )
                totals = parts if totals is None else [a + b for a, b in zip(totals, parts)]
            query_grad[rows, lanes] = (totals[0] * SCALE).astype(BF16)
            key_grad[rows, lanes] = (totals[1] * SCALE).astype(BF16)
            value_grad[rows, lanes] = totals[2].astype(BF16)
        return carry

    lax.fori_loop(0, query.shape[0] // ROWS, image, 0)


def project_back_kernel(
    query_grad,
    key_grad,
    value_grad,
    hidden,
    tok,
    resid_grad,
    vec,
    w_query,
    w_key,
    w_value,
    tokens_grad,
    w_grads,
    sums,
):
    normed = hidden[...]
    grads = (query_grad[...], key_grad[...], value_grad[...])
    for i in range(3):
        w_grads[i] = dot_tn(normed, grads[i]).astype(BF16)
    grad = dot_nt(grads[0], w_query[...]) + dot_nt(grads[1], w_key[...])
    grad = grad + dot_nt(grads[2], w_value[...])
    unit, rstd = unit_rows(tok[...].astype(F32))
    sums[0:1, :] = jnp.sum(grad * unit, 0, keepdims=True)
    sums[1:2, :] = jnp.sum(grad, 0, keepdims=True)
    sums[2:3, :] = jnp.sum(grads[0].astype(F32), 0, keepdims=True)
    sums[3:4, :] = jnp.sum(grads[2].astype(F32), 0, keepdims=True)
    tokens_grad[...] = resid_grad[...] + norm_back(grad, unit, rstd, row_of(vec, GAIN_ONE))


def mix_kernel(y_cells, cell_cols, gates, resid, mixed):
    total = resid[...]
    for k in range(2):
        hit = jnp.where(lane_hits(cell_cols, k), 1.0, 0.0).astype(BF16)
        total = total + gates[:, k : k + 1] * dot(hit, y_cells[...])
    mixed[...] = total.astype(BF16)


def exchange_near(parts, n):
    return swap(jnp.stack([parts[2], parts[3]]), n, group_mask(2))


def exchange_core(parts, from_near, n):
    from_core = swap(jnp.stack([parts[1], from_near[1]]), n, group_mask(1))
    return [parts[0], from_core[0], from_near[0], from_core[1]]


CHUNK = 768
TILE = 256


def expert_kernel(labels, me_ref, *refs):
    n_pieces = len(labels)
    pieces = refs[:n_pieces]
    blocks, cot, b_in, b_exit, y_out, block_grad, b_in_grad, b_exit_grad = refs[
        n_pieces : n_pieces + 8
    ]
    refs = refs[n_pieces + 8 :]
    n_grads = len(refs) - 10
    grads = refs[:n_grads]
    (
        w_in,
        w_exit,
        exit_grad,
        activ,
        inner_grad,
        y_sum,
        block_sum,
        load_sems,
        in_sems,
        out_sems,
    ) = refs[n_grads:]
    step = pl.program_id(0)
    steps = pl.num_programs(0)
    rows = blocks.shape[0]
    chunks = w_in.shape[1] // CHUNK

    def units(arrays, names):
        number = 0
        for array, labels_here in zip(arrays, names, strict=True):
            for i, mask in enumerate(labels_here):
                pair = 0 if mask is None else (me_ref[0] ^ mask) >> 1
                yield number, array.at[i], pair, array.shape[1] // (2 * chunks)
                number += 1

    def in_place(block, pair, count, at):
        start = pl.multiple_of(pair * count, count)
        columns = pl.ds(pl.multiple_of(at * CHUNK, CHUNK), CHUNK)
        row = pl.multiple_of(at * count, count)
        return block.at[pl.ds(row, count)], w_in.at[pl.ds(start, count), columns]

    def out_place(block, pair, count):
        start = pl.multiple_of(pair * count * chunks, count * chunks)
        return (
            block.at[pl.ds(count * chunks, count * chunks)],
            w_exit.at[pl.ds(start, count * chunks)],
        )

    def loads():
        found = []
        for number, block, pair, count in units(pieces, labels):
            for at in range(chunks):
                found.append(
                    pltpu.make_async_copy(
                        *in_place(block, pair, count, at), load_sems.at[at, number]
                    )
                )
            found.append(
                pltpu.make_async_copy(*out_place(block, pair, count), load_sems.at[chunks, number])
            )
        return found

    def in_stores(at):
        return [
            pltpu.make_async_copy(*in_place(block, pair, count, at)[::-1], in_sems.at[at, number])
            for number, block, pair, count in units(grads, GRAD_LABELS if n_pieces > 1 else labels)
        ]

    def out_stores():
        return [
            pltpu.make_async_copy(*out_place(block, pair, count)[::-1], out_sems.at[number])
            for number, block, pair, count in units(grads, GRAD_LABELS if n_pieces > 1 else labels)
        ]

    @pl.when(step == 0)
    def _():
        arriving = loads()
        for copy in arriving:
            copy.start()
        square = (CELLS, CELLS)
        same = lax.broadcasted_iota(jnp.int32, square, 0) == lax.broadcasted_iota(
            jnp.int32, square, 1
        )
        first = CAP // 16 * 16
        note = lax.broadcasted_iota(jnp.int32, (CELLS, CELLS - first), 1) + first
        for member in range(rows // CELLS):
            at = pl.ds(member * CELLS, CELLS)
            spare = blocks[pl.ds(member * CELLS + first, CELLS - first), :CELLS]
            columns = dot_nt(jnp.where(same, 1.0, 0.0).astype(BF16), spare)
            share = jnp.sum(
                jnp.where((note >= CAP) & (note < CAP + 3), columns, 0.0), -1, keepdims=True
            )
            exit_grad[at, :] = (share * cot[at, :].astype(F32)).astype(BF16)
        b_exit_grad[...] = jnp.sum(exit_grad[...].astype(F32), 0, keepdims=True)
        y_sum[...] = jnp.zeros_like(y_sum)
        block_sum[...] = jnp.zeros_like(block_sum)
        for copy in arriving:
            copy.wait()

    columns = pl.ds(pl.multiple_of(step * CHUNK, CHUNK), CHUNK)
    b_in_grad[...] = jnp.zeros_like(b_in_grad)

    def tile(i, carry):
        at = pl.ds(pl.multiple_of(i * TILE, TILE), TILE)
        w_in_part = w_in[:, columns]
        w_exit_part = w_exit[columns, :]
        inner = jnp.dot(blocks[at, :], w_in_part, preferred_element_type=F32) + b_in[...]
        square = inner * inner
        curve = jnp.tanh(0.7978845608 * (inner + 0.044715 * square * inner))
        half = 0.5 * (1.0 + curve)
        activ_tile = (half * inner).astype(BF16)
        slope = half + 0.5 * inner * (1.0 - curve * curve) * (
            0.7978845608 + (0.7978845608 * 3.0 * 0.044715) * square
        )
        activ[at, :] = activ_tile
        y_sum[at, :] += jnp.dot(activ_tile, w_exit_part, preferred_element_type=F32)
        activ_grad = lax.dot_general(
            exit_grad[at, :], w_exit_part, (((1,), (1,)), ((), ())), preferred_element_type=F32
        )
        grad_tile = (activ_grad * slope).astype(BF16)
        inner_grad[at, :] = grad_tile
        b_in_grad[...] += jnp.sum(grad_tile.astype(F32), 0, keepdims=True)
        block_sum[at, :] += lax.dot_general(
            grad_tile, w_in_part, (((1,), (1,)), ((), ())), preferred_element_type=F32
        )
        return carry

    lax.fori_loop(0, rows // TILE, tile, 0)
    w_in[:, columns] = lax.dot_general(
        blocks[...], inner_grad[...], (((0,), (0,)), ((), ())), preferred_element_type=F32
    ).astype(BF16)
    for copy in in_stores(step):
        copy.start()
    w_exit[columns, :] = lax.dot_general(
        activ[...], exit_grad[...], (((0,), (0,)), ((), ())), preferred_element_type=F32
    ).astype(BF16)

    @pl.when(step == steps - 1)
    def _():
        for copy in out_stores():
            copy.start()
        whole_y = y_sum[...] + b_exit[...]
        y_out[...] = whole_y.astype(BF16)
        block_grad[...] = block_sum[...].astype(BF16)
        dots = lax.dot_general(
            jnp.ones((8, D), F32),
            whole_y * cot[...].astype(F32),
            (((1,), (1,)), ((), ())),
            precision=lax.Precision.HIGHEST,
            preferred_element_type=F32,
        )[:1]
        thirds = []
        for _ in range(3):
            thirds.append(dots.astype(BF16).astype(F32))
            dots = dots - thirds[-1]
        write_notes(block_grad, jnp.concatenate(thirds, 0))
        for at in range(chunks):
            for copy in in_stores(at):
                copy.wait()
        for copy in out_stores():
            copy.wait()


X, Y, Z, NEAR = 2, 4, 16, 1 << GROUP_BITS[1]
GRAD_LABELS = tuple(
    tuple(mask | part for mask in masks)
    for part, (one, two) in ((0, (Y, X)), (NEAR, (X, Y)))
    for masks in ((one | two | Z,), (one | Z,), (one, one | two), (Z, two | Z), (0, two))
)


def run_expert(pieces, labels, me, blocks, cot, b_in, b_exit):
    rows = blocks.shape[0]
    ff = b_in.shape[1]
    chunks = ff // CHUNK
    any_spec = pl.BlockSpec(memory_space=pl.ANY)
    n_units = sum(len(names) for names in labels)
    if len(pieces) > 1:
        grad_shapes = [(len(names),) + pieces[0].shape[1:] for names in GRAD_LABELS]
    else:
        grad_shapes = [pieces[0].shape]

    def whole(shape):
        return pl.BlockSpec(shape, lambda i: (0,) * len(shape))

    results = pl.pallas_call(
        functools.partial(expert_kernel, labels),
        grid=(chunks,),
        out_shape=[
            jax.ShapeDtypeStruct((rows, D), BF16),
            jax.ShapeDtypeStruct((rows, D), BF16),
            jax.ShapeDtypeStruct((1, ff), F32),
            jax.ShapeDtypeStruct((1, D), F32),
        ]
        + [jax.ShapeDtypeStruct(shape, BF16) for shape in grad_shapes],
        in_specs=[pl.BlockSpec(memory_space=pltpu.SMEM)]
        + [any_spec] * len(pieces)
        + [
            whole((rows, D)),
            whole((rows, D)),
            pl.BlockSpec((1, CHUNK), lambda i: (0, i)),
            whole((1, D)),
        ],
        out_specs=[
            whole((rows, D)),
            whole((rows, D)),
            pl.BlockSpec((1, CHUNK), lambda i: (0, i)),
            whole((1, D)),
        ]
        + [any_spec] * len(grad_shapes),
        scratch_shapes=[
            pltpu.VMEM((D, ff), BF16),
            pltpu.VMEM((ff, D), BF16),
            pltpu.VMEM((rows, D), BF16),
            pltpu.VMEM((rows, CHUNK), BF16),
            pltpu.VMEM((rows, CHUNK), BF16),
            pltpu.VMEM((rows, D), F32),
            pltpu.VMEM((rows, D), F32),
            pltpu.SemaphoreType.DMA((chunks + 1, n_units)),
            pltpu.SemaphoreType.DMA((chunks, n_units)),
            pltpu.SemaphoreType.DMA((n_units,)),
        ],
        compiler_params=pltpu.CompilerParams(
            vmem_limit_bytes=58 * 2**20, dimension_semantics=("arbitrary",)
        ),
    )(me.reshape(1).astype(jnp.int32), *pieces, blocks, cot, b_in, b_exit)
    return results[:4], list(results[4:])


def group_pieces(parts, me):
    high = bit_of(me, GROUP_BITS[0]) == 1
    rows = parts[0].shape[0] // 8

    def pair(first, second):
        def part(low, count):
            here, there = first[low : low + count], second[low : low + count]
            here = here.reshape(-1, 1, count // 4 if low == 0 else count, D)
            there = there.reshape(here.shape)
            return jnp.concatenate(
                [jnp.where(high, there, here), jnp.where(high, here, there)], 1
            ).reshape(2 * count, D)

        return jnp.concatenate([part(0, 4 * rows), part(4 * rows, 4 * rows)])[None]

    return pair(parts[0], parts[1]), pair(parts[2], parts[3])


def expert_gather_rest(sent, n, me):
    by_mask = {0: sent[0], NEAR: sent[1]}
    for bit in range(n.bit_length() - 1):
        if bit not in GROUP_BITS:
            for mask in list(by_mask):
                by_mask[mask | 1 << bit] = swap(by_mask[mask], n, 1 << bit)
    order = (jnp.arange(n // 2, dtype=jnp.int32) ^ (me >> 1))
    blocks = jnp.take(
        jnp.concatenate([by_mask[2 * pair] for pair in range(n // 2)]), order, axis=0
    )
    rows = blocks.shape[1] // 16
    w_in = blocks[:, : 8 * rows].reshape(n // 2, 4, 2 * rows, D)
    w_in = w_in.transpose(1, 0, 2, 3).reshape(4 * n * rows, D)
    return [jnp.concatenate([w_in, blocks[:, 8 * rows :].reshape(-1, D)])[None]], ((None,),)


def add(*terms):
    total = terms[0].astype(F32)
    for term in terms[1:]:
        total = total + term.astype(F32)
    return total.astype(BF16)


def expert_scatter_rest(grads, n, me):
    whole = grads[0][0]
    rows = whole.shape[0] // (8 * n)
    half = whole.shape[0] // 2
    w_in = whole[:half].reshape(4, n // 2, 2 * rows, D).transpose(1, 0, 2, 3)
    w_in = w_in.reshape(n // 2, 8 * rows, D)
    x = jnp.concatenate([w_in, whole[half:].reshape(n // 2, 8 * rows, D)], 1)
    width = n.bit_length() - 1
    x = x.reshape((2,) * (width - 1) + (16 * rows, D))
    for bit in range(1, width):
        if bit not in GROUP_BITS:
            x = halve(x, n, me, bit, width - 1 - bit)
    x = x.reshape(2, 16 * rows, D)
    near = bit_of(me, GROUP_BITS[1])
    return [lax.dynamic_index_in_dim(x, near ^ k, 0, keepdims=False) for k in range(2)]


def expert_scatter(sums, n, me):
    high = bit_of(me, GROUP_BITS[0]) == 1
    half = sums[0].shape[0] // 2

    def side(total, k):
        w_in = total[:half].reshape(4, 2, half // 8, D)
        w_exit = total[half:].reshape(2, half // 2, D)
        return jnp.concatenate(
            [
                jnp.where(high, w_in[:, 1 - k], w_in[:, k]).reshape(half // 2, D),
                jnp.where(high, w_exit[1 - k], w_exit[k]),
            ]
        )

    sides = [side(sums[k >> 1], k & 1) for k in range(EXP)]
    from_core = swap(jnp.stack([sides[1], sides[3]]), n, group_mask(1))
    from_near = swap(jnp.stack([sides[2], from_core[1]]), n, group_mask(2))
    return [sides[0], from_core[0], from_near[0], from_near[1]]


def per_device(
    n,
    tokens,
    cotangent,
    expert_ids,
    slots,
    norm1_gain,
    norm1_shift,
    query_weight,
    query_bias,
    key_weight,
    value_weight,
    value_bias,
    out_weight,
    out_bias,
    norm2_gain,
    norm2_shift,
    router_weight,
    expert_in,
    expert_in_bias,
    expert_out,
    expert_out_bias,
):
    me = lax.axis_index(AXIS)
    width = n.bit_length() - 1
    tuned = n == 32
    expert = bit_of(me, GROUP_BITS[0]) | bit_of(me, GROUP_BITS[1]) << 1
    far_bits = [b for b in range(width) if b not in GROUP_BITS and b > 2][::-1]
    rows = query_weight.shape[0]
    ff_rows = expert_out.shape[1]
    ff = ff_rows * n
    images = tokens.shape[0] // SEQ
    t_rows = images * ROWS

    def pad_images(x, value=0):
        x = x.reshape(images, SEQ, x.shape[1])
        x = jnp.pad(x, ((0, 0), (0, ROWS - SEQ), (0, 0)), constant_values=value)
        return x.reshape(t_rows, x.shape[2])

    def cut_images(x):
        return x.reshape(images, ROWS, D)[:, :SEQ].reshape(images * SEQ, D)

    vectors = jnp.stack(
        [norm1_gain, norm1_shift, query_bias, value_bias, out_bias, norm2_gain, norm2_shift]
    )
    small = jnp.concatenate([vectors, router_weight.T, expert_out_bias], 0).reshape(-1)
    small = jnp.concatenate([small, expert_in_bias.reshape(-1)])
    n_small = small.shape[0]
    small = jnp.pad(small, (0, D - n_small)).reshape(1, D)
    in_chunks = expert_in.reshape(EXP, rows, 4, D).transpose(0, 2, 1, 3).reshape(EXP, 4 * rows, D)
    shards = jnp.concatenate([in_chunks, expert_out], 1)
    shards = [
        lax.dynamic_index_in_dim(shards, expert ^ k, 0, keepdims=False) for k in range(EXP)
    ]
    pack_a = jnp.concatenate([query_weight, key_weight], 0)
    pack_b = jnp.concatenate([value_weight, out_weight, jnp.pad(small, ((0, 7), (0, 0)))], 0)
    full_a = pack_a.reshape((1,) * width + pack_a.shape)
    full_b = pack_b.reshape((1,) * width + pack_b.shape)
    shards_near = exchange_near(shards, n)
    for bit in far_bits + [3]:
        full_a = gather_step(full_a, n, me, bit)
        full_b = gather_step(full_b, n, me, bit)
    full_a, full_b, shards_near = gate([full_a, full_b, shards_near])
    full_a = gather_step(full_a, n, me, 1)
    full_b = gather_step(full_b, n, me, 2)
    in_group = exchange_core(shards, shards_near, n)
    full_a, full_b = gate([full_a, full_b], in_group[3])
    halves = group_pieces(in_group, me)
    full_a = gather_step(full_a, n, me, 2)
    full_b = gather_step(full_b, n, me, 1)
    full = jnp.concatenate([full_a, full_b], -2)
    if tuned:
        far_0 = swap(halves[0], n, Z)
        first = [swap(half, n, one) for half, one in zip(halves, (X, Y))]
        full, *first = gate([full, *first])
    full = gather_step(full, n, me, 0).reshape((n, 4 * rows + 8, D))
    w_query, w_key, w_value, w_out = [
        full[:, i * rows : (i + 1) * rows].reshape(D, D) for i in range(4)
    ]
    small_full = full[:, 4 * rows]
    vec = small_full[:, : 15 * rows].reshape(n, 15, rows).transpose(1, 0, 2).reshape(15, D)
    vec_f32 = vec[:8].astype(F32)
    w_router = jnp.pad(vec[7:11], ((0, LANES - EXP), (0, 0)))
    b_exit = lax.dynamic_index_in_dim(vec[11:15], expert, 0, keepdims=True).astype(F32)
    b_in_all = small_full[:, 15 * rows : n_small].reshape(n, EXP, ff_rows)
    b_in = lax.dynamic_index_in_dim(b_in_all, expert, 1, keepdims=False).reshape(1, ff).astype(F32)

    tok = pad_images(tokens)
    cot = pad_images(cotangent)
    id_cols = pad_images(expert_ids, -1)
    cell_cols = pad_images((expert_ids ^ expert) * CELLS + slots, -1)
    cell_ids = jnp.arange(EXP * CELLS, dtype=jnp.int32)
    cell_rows = cell_cols.T
    spread = (cell_rows[:1] == cell_ids[:, None]) | (cell_rows[1:] == cell_ids[:, None])
    cot_cells = jnp.dot(spread.astype(BF16), cot, preferred_element_type=F32).astype(BF16)

    wide = ((t_rows, D), BF16)
    wide_f32 = ((t_rows, D), F32)
    hidden_a, query, keys, values, passed = call(
        project_kernel,
        [wide] * 4,
        [tok, vec_f32, w_query, w_key, w_value],
        [cot_cells] + ([halves[1], far_0] if tuned else []),
    )
    cot_parts = passed[0].reshape(EXP, CELLS, D)
    cot_near = exchange_near(cot_parts, n)
    pieces, labels = [], []
    if tuned:
        halves = [halves[0], passed[1]]
        far_0 = passed[2]
        far_1 = swap(halves[1], n, Z)
        both = [
            swap(jnp.concatenate([half, got]), n, X ^ Y ^ one)
            for half, got, one in zip(halves, first, (X, Y))
        ]
        pieces += [halves[0], first[0], halves[1], first[1], *both]
        labels += [(0,), (X,), (NEAR,), (NEAR | Y,), (Y, X | Y), (NEAR | X, NEAR | X | Y)]
    attended, resid, hidden_b, gates, cells, _ = call(
        attend_kernel,
        [wide, wide_f32, wide, ((t_rows, LANES), F32), ((EXP * CELLS, D), BF16)],
        [query, keys, values, tok, vec_f32, w_out, w_router, id_cols, cell_cols],
    )
    cell_parts = cells.reshape(EXP, CELLS, D)
    cells_near = exchange_near(cell_parts, n)
    if tuned:
        cells_near, cot_near, far_0, far_1 = gate([cells_near, cot_near, far_0, far_1], *both)
        far_got_0 = swap(far_0, n, X)
        far_got_1 = swap(far_1, n, Y)
        far_both_0 = swap(jnp.concatenate([far_0, far_got_0]), n, Y)
        far_both_1 = swap(jnp.concatenate([far_1, far_got_1]), n, X)
        pieces += [far_0, far_got_0, far_both_0, far_1, far_got_1, far_both_1]
        labels += [
            (Z,),
            (Z | X,),
            (Z | Y, Z | X | Y),
            (NEAR | Z,),
            (NEAR | Z | Y,),
            (NEAR | Z | X, NEAR | Z | X | Y),
        ]
        labels = tuple(labels)
    else:
        pieces, labels = expert_gather_rest(halves, n, me)

    blocks = jnp.concatenate(exchange_core(cell_parts, cells_near, n))
    cot_blocks = jnp.concatenate(exchange_core(cot_parts, cot_near, n))
    (expert_y, block_grad, b_in_grad, b_exit_grad), w_grads = run_expert(
        pieces, labels, me, blocks, cot_blocks, b_in, b_exit
    )

    grad_parts = block_grad.reshape(EXP, CELLS, D)
    grad_near = exchange_near(grad_parts, n)
    ones = ((0, Y), (5, X))
    if tuned:
        first = [swap(w_grads[at], n, one) for at, one in ones]
        grad_near, w_grads[1], w_grads[6], *first = gate(
            [grad_near, w_grads[1], w_grads[6], *first]
        )
        across = [
            swap(add(w_grads[at + 3][1], got[0]), n, X ^ Y ^ one)
            for (at, one), got in zip(ones, first)
        ]
        straight = [swap(w_grads[at + 1], n, one) for at, one in ones]
    grad_cells = jnp.concatenate(exchange_core(grad_parts, grad_near, n))
    resid_grad, attended_grad, w_out_grad, router_grad, sums_two, passed = call(
        branch_back_kernel,
        [wide_f32, wide, ((D, D), BF16), ((8, D), F32), ((8, D), F32)],
        [
            grad_cells,
            id_cols,
            cell_cols,
            gates,
            hidden_b,
            attended,
            resid,
            cot,
            vec_f32,
            w_router,
            w_out,
        ],
    )
    query_grad, key_grad, value_grad, passed = call(
        attend_back_kernel,
        [wide] * 3,
        [query, keys, values, attended_grad],
        [expert_y] + ([w_grads[2], w_grads[7]] if tuned else []),
    )
    y_parts = passed[0].reshape(EXP, CELLS, D)
    if tuned:
        query_grad, y_parts, w_grads[2], w_grads[7], *got = gate(
            [query_grad, y_parts, *passed[1:], *across, *straight]
        )
        across, straight = got[:2], got[2:]
        far = jnp.concatenate(
            [
                add(w_grads[at + 3][0], got, over)
                for (at, one), got, over in zip(ones, straight, across)
            ]
        )
        far = swap(far, n, Z)
        second = [swap(w_grads[at + 2], n, one) for at, one in ones]
    y_near = exchange_near(y_parts, n)
    tokens_grad, qkv_grad, sums_one, _ = call(
        project_back_kernel,
        [wide_f32, ((3, D, D), BF16), ((8, D), F32)],
        [
            query_grad,
            key_grad,
            value_grad,
            hidden_a,
            tok,
            resid_grad,
            vec_f32,
            w_query,
            w_key,
            w_value,
        ],
    )
    y_cells = jnp.concatenate(exchange_core(y_parts, y_near, n))
    (mixed_out, _) = call(mix_kernel, [wide], [y_cells, cell_cols, gates, resid])

    own_expert = (jnp.arange(EXP, dtype=jnp.int32) == expert)[:, None]
    vec_grad = jnp.concatenate(
        [
            sums_one[:4],
            sums_two[2:3],
            sums_two[:2],
            router_grad[:EXP],
            jnp.where(own_expert, b_exit_grad, 0.0),
        ],
        0,
    ).astype(BF16)
    vec_grad = vec_grad.reshape(15, n, rows).transpose(1, 0, 2).reshape(n, 15 * rows)
    in_grad = jnp.where(own_expert, b_in_grad, 0.0).astype(BF16)
    in_grad = in_grad.reshape(EXP, n, ff_rows).transpose(1, 0, 2).reshape(n, EXP * ff_rows)
    small_grad = jnp.pad(
        jnp.concatenate([vec_grad, in_grad], 1), ((0, 0), (0, D - n_small))
    ).reshape(n, 1, D)
    small_grad = jnp.pad(small_grad, ((0, 0), (0, 7), (0, 0)))
    qkv_rows = [qkv_grad[i].reshape(n, rows, D) for i in range(3)]
    qkv_rows += [w_out_grad.reshape(n, rows, D), small_grad]
    sums = split_owners(jnp.concatenate(qkv_rows, 1), n)
    (sums,) = sum_step([sums], n, me, [0])
    sum_a, sum_b = sums[..., : 2 * rows, :], sums[..., 2 * rows :, :]
    for bit in (1, 2):
        (sum_a,) = sum_step([sum_a], n, me, [bit])
        (sum_b,) = sum_step([sum_b], n, me, [3 - bit])
    sums = jnp.concatenate([sum_a, sum_b], -2)
    for at in range(3, width, 2):
        (sums,) = sum_step([sums], n, me, list(range(at, min(at + 2, width))))
    sums = sums.reshape(4 * rows + 8, D).astype(F32)

    if tuned:
        near = [
            swap(add(w_grads[at + 4][1], got[1]), n, X ^ Y ^ one)
            for (at, one), got in zip(ones, second)
        ]
        w_sums = [
            add(w_grads[at + 4][0], two[0], beside, far[i])
            for i, ((at, one), two, beside) in enumerate(zip(ones, second, near))
        ]
    else:
        w_sums = expert_scatter_rest(w_grads, n, me)
    w_sums = expert_scatter(w_sums, n, me)
    places = jnp.arange(EXP, dtype=jnp.int32) ^ expert
    w_sums = jnp.stack([lax.select_n(places[i], *w_sums) for i in range(EXP)]).astype(F32)
    w_in_sum = w_sums[:, : 4 * rows].reshape(EXP, 4, rows, D).transpose(0, 2, 1, 3)
    w_in_sum = w_in_sum.reshape(EXP, rows, ff)
    w_exit_sum = w_sums[:, 4 * rows :]

    small_sum = sums[4 * rows]
    vec_sum = small_sum[: 15 * rows].reshape(15, rows)
    b_in_sum = small_sum[15 * rows : n_small].reshape(EXP, ff_rows)
    return (
        cut_images(mixed_out),
        cut_images(tokens_grad),
        vec_sum[GAIN_ONE],
        vec_sum[SHIFT_ONE],
        sums[:rows],
        vec_sum[B_QUERY],
        sums[rows : 2 * rows],
        sums[2 * rows : 3 * rows],
        vec_sum[B_VALUE],
        sums[3 * rows : 4 * rows],
        vec_sum[B_OUT],
        vec_sum[GAIN_TWO],
        vec_sum[SHIFT_TWO],
        vec_sum[7:11].T,
        w_in_sum,
        b_in_sum,
        w_exit_sum,
        vec_sum[11:15],
    )


def solution(mesh):
    in_specs = (
        P("fsdp", None),
        P("fsdp", None),
        P("fsdp", None),
        P("fsdp", None),
        P("fsdp"),
        P("fsdp"),
        P("fsdp", None),
        P("fsdp"),
        P("fsdp", None),
        P("fsdp", None),
        P("fsdp"),
        P("fsdp", None),
        P("fsdp"),
        P("fsdp"),
        P("fsdp"),
        P("fsdp", None),
        P(None, "fsdp", None),
        P(None, "fsdp"),
        P(None, "fsdp", None),
        P(None, "fsdp"),
    )
    out_specs = (
        P("fsdp", None),
        P("fsdp", None),
        P("fsdp"),
        P("fsdp"),
        P("fsdp", None),
        P("fsdp"),
        P("fsdp", None),
        P("fsdp", None),
        P("fsdp"),
        P("fsdp", None),
        P("fsdp"),
        P("fsdp"),
        P("fsdp"),
        P("fsdp", None),
        P(None, "fsdp", None),
        P(None, "fsdp"),
        P(None, "fsdp", None),
        P(None, "fsdp"),
    )
    return jax.shard_map(
        functools.partial(per_device, mesh.shape["fsdp"]),
        mesh=mesh,
        in_specs=in_specs,
        out_specs=out_specs,
        check_vma=False,
    )
```
